32 devices in a mesh: cols: 2 (over x), sites: 16 (over z, y, core).
Axes of the slice: x: 2, y: 2, z: 4, core: 2. Of those that a mesh axis runs over, the one named last changes fastest.
Arguments:
- right_vectors: float32 [2, 64, 2, 16, 32, 256], P(None, None, None, None, ('cols', 'sites')), may hold values from -6 to 6
- left_vectors: bfloat16 [2, 64, 256, 512], P(None, None, 'sites'), may hold values from -0.015625 to 0.015625
- vacancy: int32 [256, 512], P('sites'), may hold values 0 or 1
Outputs:
- gamma_moments: float32 [2, 4, 64, 64, 2], P(None, None, None, None, 'cols')
The draws below stay inside these ranges and needn't reach their ends.
All inputs are finite; a program needn't handle non-finite values. No bound on the sum of `vacancy` on one device may be relied on, other than what follows from the above.
Results may differ from the reference program's by a relative error of at most 0.0029.
Values sent between devices are 32-bit elements; how exact they have to be, the bound alone decides.
A program may use at most 128 MiB of HBM per device.

```python
import jax
import jax.numpy as jnp
from jax import lax

COLS = 128
NL = 64
MOM = 4
LX = 512
RS = 16
LY = 256
CG = 64
PIECE = 256


def touch_ends(drawn, key, least, high):
    longest = drawn.shape.index(max(drawn.shape))
    spots = []
    for shift in (0, 1):
        where = [jax.random.randint(jax.random.fold_in(key, axis), (), 0, length) for axis, length in enumerate(drawn.shape)]
        where[longest] = (where[longest] + shift) % drawn.shape[longest]
        spots.append(tuple(where))
    return drawn.at[spots[0]].set(least).at[spots[1]].set(high)


def level_of(own_key, extent, pieces, least, top_value):
    loudness, own = 1.0, jax.random.fold_in(own_key, 6)
    for axis_at, blocks in pieces:
        steps = jnp.exp(jax.random.uniform(jax.random.fold_in(own, axis_at), (blocks,), jnp.float32, least / len(pieces), top_value / len(pieces)))
        loudness = loudness * jnp.repeat(steps, extent[axis_at] // blocks).reshape([-1 if axis == axis_at else 1 for axis in range(len(extent))])
    return loudness


def gaussian(key, extent, spread, limit, pieces=(), held_as=jnp.bfloat16):
    gain = level_of(key, extent, pieces, -0.22, 0.18) if pieces else 1.0
    entries = jax.random.normal(key, extent, jnp.float32) * spread * gain
    return jnp.minimum(jnp.maximum(entries, -limit), limit).astype(held_as)


def setup_inputs(seed: int = 0) -> dict:
    streams_of = jax.random.split(jax.random.key(seed), 4)
    return {
        "right_vectors": gaussian(streams_of[0], (2, CG, COLS // CG, LY // RS, (COLS // CG) * (LY // RS), PIECE), 1.0, 6.0, ((4, 32),), jnp.float32),
        "left_vectors": gaussian(streams_of[1], (2, NL, LY, LX), (LY * LX) ** -0.5, 0.015625, ((2, 16),)),
        "vacancy": touch_ends((jax.random.randint(streams_of[2], (LY, LX), 0, 16) < 15).astype(jnp.int32), jax.random.fold_in(streams_of[2], 1), 0, 1),
    }


ONSITE_MASS = 0.3
SECOND_HOP = 0.2
BAND_SCALE = 4.5


def column_shift(values, offset):
    row_width = values.shape[-1]
    filler = jnp.zeros(values.shape[:-1] + (abs(offset),), values.dtype)
    if offset > 0:
        return jnp.concatenate([values[..., offset:], filler], axis=-1)
    return jnp.concatenate([filler, values[..., :row_width + offset]], axis=-1)


def rotate_phase(values):
    return jnp.stack([-values[1], values[0]])


def sign_table(row_count, row_width):
    rows_index = lax.broadcasted_iota(jnp.int32, (row_count, row_width), 0)
    cols_index = lax.broadcasted_iota(jnp.int32, (row_count, row_width), 1)
    return (1 - 2 * ((rows_index + cols_index) % 2)).astype(jnp.float32)


def haldane(padded, parity_sign):
    centre = padded[:, :, 1:-1, :]
    upper_row = padded[:, :, 2:, :]
    lower_row = padded[:, :, :-2, :]
    vertical = jnp.where(parity_sign > 0, upper_row, lower_row)
    nearest = column_shift(centre, 1) + column_shift(centre, -1) + vertical
    second = (column_shift(centre, 2) - column_shift(centre, -2) + column_shift(upper_row, -1)
              - column_shift(lower_row, 1) + column_shift(lower_row, -1) - column_shift(upper_row, 1))
    return ONSITE_MASS * parity_sign * centre + nearest + SECOND_HOP * parity_sign * rotate_phase(second)


def velocity(padded, parity_sign):
    centre = padded[:, :, 1:-1, :]
    upper_row = padded[:, :, 2:, :]
    lower_row = padded[:, :, :-2, :]
    along_x = column_shift(centre, 1) - column_shift(centre, -1)
    farther = column_shift(centre, 2) + column_shift(centre, -2)
    diagonal = (column_shift(upper_row, 1) + column_shift(upper_row, -1)
                + column_shift(lower_row, 1) + column_shift(lower_row, -1))
    return rotate_phase(along_x) - SECOND_HOP * parity_sign * (2.0 * farther - diagonal)


def wrap_rows(values):
    return jnp.concatenate([values[:, :, -1:, :], values, values[:, :, :1, :]], axis=2)


def reference(right_vectors, left_vectors, vacancy):
    group_count = COLS // CG
    columns = jnp.moveaxis(right_vectors.reshape(2, CG, group_count, LY, LX), 2, 0)
    present = vacancy.astype(jnp.float32)
    parity_sign = sign_table(LY, LX)
    left_matrix = left_vectors.astype(jnp.float32).reshape(2 * NL, LY * LX)

    def one_group(column_block):
        current = column_block * present
        latest = velocity(wrap_rows(current), parity_sign) * present
        previous = latest
        moment_list = [latest]
        for degree in range(1, MOM):
            applied = haldane(wrap_rows(latest), parity_sign) * present / BAND_SCALE
            following = applied if degree == 1 else 2.0 * applied - previous
            previous, latest = latest, following
            moment_list.append(latest)
        outputs = []
        for moment in moment_list:
            rounded = lax.optimization_barrier(moment.astype(jnp.bfloat16)).astype(jnp.float32)
            product = lax.dot_general(left_matrix, rounded.reshape(2 * CG, LY * LX),
                                      (((1,), (1,)), ((), ())),
                                      precision=lax.Precision.HIGHEST,
                                      preferred_element_type=jnp.float32).reshape(2, NL, 2, CG)
            outputs.append(jnp.stack([product[0, :, 0] + product[1, :, 1],
                                      product[0, :, 1] - product[1, :, 0]]))
        return jnp.stack(outputs, axis=1)

    gathered = lax.map(one_group, columns)
    return jnp.moveaxis(gathered, 0, -1)
```

```python
import functools

import jax
import jax.numpy as jnp
from jax import lax
from jax.experimental import pallas as pl
from jax.experimental.pallas import tpu as pltpu
from jax.sharding import PartitionSpec as P

MOM = 4


ONSITE_MASS = 0.3
SECOND_HOP = 0.2
BAND_SCALE = 4.5


def padded_2(cells, sides, width):
    for axis, dim in sides:
        count = lax.axis_size(axis)
        head = lax.slice_in_dim(cells, 0, width, axis=dim)
        tail = lax.slice_in_dim(cells, cells.shape[dim] - width, cells.shape[dim], axis=dim)
        cells = jnp.concatenate(
            [
                lax.ppermute(tail, axis, [(i, (i + 1) % count) for i in range(count)]),
                cells,
                lax.ppermute(head, axis, [((i + 1) % count, i) for i in range(count)]),
            ],
            axis=dim,
        )
    return cells


def column_shift(values, offset):
    row_width = values.shape[-1]
    filler = jnp.zeros(values.shape[:-1] + (abs(offset),), values.dtype)
    if offset > 0:
        return jnp.concatenate([values[..., offset:], filler], axis=-1)
    return jnp.concatenate([filler, values[..., : row_width + offset]], axis=-1)


def rotate_phase(values):
    return jnp.stack([-values[1], values[0]])


def sign_table(row_count, row_width):
    rows_index = lax.broadcasted_iota(jnp.int32, (row_count, row_width), 0)
    cols_index = lax.broadcasted_iota(jnp.int32, (row_count, row_width), 1)
    return (1 - 2 * ((rows_index + cols_index) % 2)).astype(jnp.float32)


def haldane(padded, parity_sign):
    centre = padded[:, :, 1:-1, :]
    upper_row = padded[:, :, 2:, :]
    lower_row = padded[:, :, :-2, :]
    vertical = jnp.where(parity_sign > 0, upper_row, lower_row)
    nearest = column_shift(centre, 1) + column_shift(centre, -1) + vertical
    second = (
        column_shift(centre, 2)
        - column_shift(centre, -2)
        + column_shift(upper_row, -1)
        - column_shift(lower_row, 1)
        + column_shift(lower_row, -1)
        - column_shift(upper_row, 1)
    )
    return (
        ONSITE_MASS * parity_sign * centre
        + nearest
        + SECOND_HOP * parity_sign * rotate_phase(second)
    )


def velocity(padded, parity_sign):
    centre = padded[:, :, 1:-1, :]
    upper_row = padded[:, :, 2:, :]
    lower_row = padded[:, :, :-2, :]
    along_x = column_shift(centre, 1) - column_shift(centre, -1)
    farther = column_shift(centre, 2) + column_shift(centre, -2)
    diagonal = (
        column_shift(upper_row, 1)
        + column_shift(upper_row, -1)
        + column_shift(lower_row, 1)
        + column_shift(lower_row, -1)
    )
    return rotate_phase(along_x) - SECOND_HOP * parity_sign * (2.0 * farther - diagonal)


def with_rims(values):
    return padded_2(values, (("sites", 2),), 1)


def per_device_plain(right_vectors, left_vectors, vacancy):
    layout = right_vectors.shape
    pieces = right_vectors.reshape(layout[0], layout[1], layout[2], layout[3], layout[5])
    slab_field = lax.all_to_all(
        lax.all_to_all(pieces, "cols", split_axis=2, concat_axis=2, tiled=True),
        "sites",
        split_axis=3,
        concat_axis=3,
        tiled=True,
    )
    row_count = left_vectors.shape[2]
    row_width = left_vectors.shape[3]
    count_left = left_vectors.shape[1]
    group_width = layout[1]
    site_count = row_count * row_width
    present = vacancy.astype(jnp.float32)
    current = slab_field.reshape(2, group_width, row_count, row_width) * present
    parity_sign = sign_table(row_count, row_width)
    latest = velocity(with_rims(current), parity_sign) * present
    previous = latest
    moment_list = [latest]
    for degree in range(1, MOM):
        applied = haldane(with_rims(latest), parity_sign) * present / BAND_SCALE
        following = applied if degree == 1 else 2.0 * applied - previous
        previous, latest = (latest, following)
        moment_list.append(latest)
    left_matrix = left_vectors.reshape(2 * count_left, site_count)
    summed_list = []
    for moment in moment_list:
        rounded = moment.astype(jnp.bfloat16).reshape(2 * group_width, site_count)
        product = lax.dot_general(
            left_matrix, rounded, (((1,), (1,)), ((), ())), preferred_element_type=jnp.float32
        ).reshape(2, count_left, 2, group_width)
        combined = jnp.stack(
            [product[0, :, 0] + product[1, :, 1], product[0, :, 1] - product[1, :, 0]]
        )
        summed_list.append(lax.psum(combined, "sites"))
    summed = jnp.stack(summed_list, axis=1)
    return summed[..., None]


MESH = pl.DeviceIdType.MESH
HALO = MOM
COLS_AT_ONCE = 16


def fused_kernel(
    groups, sites, right_ref, left_ref, vacancy_ref, out_ref,
    arrived, field0, field1, field2, field3, present, scaled, doubled, rounded,
    partial, shares, total,
    piece_send, piece_recv, rim_send, rim_recv, mask_send, mask_recv,
    share_send, share_recv, total_send, total_recv,
):
    chunks, padded_rows, _, wide, width = arrived.shape
    rows = padded_rows - 2 * HALO
    piece = right_ref.shape[5]
    per_row = width // piece
    count = groups * sites
    my_group, my_site = lax.axis_index("cols"), lax.axis_index("sites")
    mine = my_group * sites + my_site
    above, below = lax.rem(my_site + 1, sites), lax.rem(my_site + sites - 1, sites)

    barrier = pltpu.get_barrier_semaphore()

    def greet(step, carry):
        other = lax.rem(mine + step, count)
        pl.semaphore_signal(
            barrier, inc=1, device_id={"cols": other // sites, "sites": lax.rem(other, sites)}, device_id_type=MESH
        )
        return carry

    lax.fori_loop(1, count, greet, 0)

    lane = lax.broadcasted_iota(jnp.int32, (8, width), 1)
    odd_lane = lax.rem(lane, 2) == 1

    for row in range(rows):
        present[HALO + row] = jnp.broadcast_to(vacancy_ref[row : row + 1, :].astype(jnp.float32), (8, width))

    pl.semaphore_wait(barrier, count - 1)

    def landing(chunk, run):
        return arrived.at[
            chunk, HALO + run // per_row, :, :, pl.ds(pl.multiple_of(lax.rem(run, per_row) * piece, piece), piece)
        ]

    def piece_of(chunk, group, site):
        return right_ref.at[:, pl.ds(pl.multiple_of(chunk * wide, wide), wide), group, site, 0, :]

    def piece_copy(chunk, step):
        other = lax.rem(mine + step, count)
        group, site = other // sites, lax.rem(other, sites)
        return pltpu.make_async_remote_copy(
            src_ref=piece_of(chunk, group, site),
            dst_ref=landing(chunk, mine),
            send_sem=piece_send.at[chunk, step],
            recv_sem=piece_recv.at[chunk],
            device_id={"cols": group, "sites": site},
            device_id_type=MESH,
        )

    def rim_copy(source, send_sem, recv_sem, up):
        first = rows if up else HALO
        landing_row = 0 if up else rows + HALO
        return pltpu.make_async_remote_copy(
            src_ref=source.at[pl.ds(first, HALO)],
            dst_ref=source.at[pl.ds(landing_row, HALO)],
            send_sem=send_sem,
            recv_sem=recv_sem,
            device_id={"sites": above if up else below},
            device_id_type=MESH,
        )

    def mask_copies():
        return [rim_copy(present, mask_send.at[i], mask_recv.at[i], up) for i, up in enumerate((True, False))]

    def rim_copies(chunk):
        return [
            rim_copy(arrived.at[chunk], rim_send.at[chunk, i], rim_recv.at[chunk, i], up)
            for i, up in enumerate((True, False))
        ]

    for copy in mask_copies():
        copy.start()

    def send_chunk(chunk, carry):
        def send(step, inner):
            piece_copy(chunk, step).start()
            return inner

        lax.fori_loop(1, count, send, 0)
        pltpu.make_async_copy(piece_of(chunk, my_group, my_site), landing(chunk, mine), piece_recv.at[chunk]).start()
        return carry

    lax.fori_loop(0, chunks, send_chunk, 0)

    for copy in mask_copies():
        copy.wait()

    def scale_masks(row, carry):
        held = present[row]
        scaled[row] = held * (1.0 / BAND_SCALE)
        doubled[row] = held * (2.0 / BAND_SCALE)
        return carry

    lax.fori_loop(0, padded_rows, scale_masks, 0)

    def shift(values, offset):
        turned = pltpu.roll(values, width - 1 if offset > 0 else 1, axis=1)
        return jnp.where(lane == (width - 1 if offset > 0 else 0), 0.0, turned)

    def signed(values, odd_row):
        return jnp.where(odd_lane != odd_row, -values, values)

    def sweep(source, target, earlier, mask, degree):
        first = degree + 1

        def one_row(row, odd_row):
            halves = [[], []]
            for part in range(0, wide, 8):
                at = slice(part, part + 8)
                centre = [source[row, r, at, :] for r in (0, 1)]
                upper = [source[row + 1, r, at, :] for r in (0, 1)]
                lower = [source[row - 1, r, at, :] for r in (0, 1)]
                right = [shift(c, 1) for c in centre]
                left = [shift(c, -1) for c in centre]
                both = [u + l for u, l in zip(upper, lower)]
                if degree == 0:
                    far = [shift(2.0 * a - s, 1) + shift(2.0 * b - s, -1) for a, b, s in zip(right, left, both)]
                    near = [a - b for a, b in zip(right, left)]
                    applied = [
                        -near[1] - signed(SECOND_HOP * far[0], odd_row),
                        near[0] - signed(SECOND_HOP * far[1], odd_row),
                    ]
                else:
                    far = [shift(a - s, 1) - shift(b - s, -1) for a, b, s in zip(right, left, both)]
                    phase = [-far[1], far[0]]
                    applied = [
                        signed(ONSITE_MASS * centre[r] + SECOND_HOP * phase[r], odd_row)
                        + (right[r] + left[r])
                        + jnp.where(odd_lane != odd_row, lower[r], upper[r])
                        for r in (0, 1)
                    ]
                factor = mask[row]
                for r in (0, 1):
                    result = applied[r] * factor
                    if earlier is not None:
                        result = result - earlier[row, r, at, :]
                    if target is not None:
                        target[row, r, at, :] = result
                    halves[r].append(result)
            lanes = pl.ds(pl.multiple_of(row * width, width), width)
            for r in (0, 1):
                base = (r * MOM + degree) * wide
                rounded[base : base + wide, lanes] = jnp.concatenate(halves[r], axis=0).astype(jnp.bfloat16)

        def pair(step, carry):
            one_row(first + 2 * step, first % 2 == 1)
            one_row(first + 2 * step + 1, first % 2 == 0)
            return carry

        lax.fori_loop(0, (padded_rows - 2 * first) // 2, pair, 0)

    def stage(chunk):
        held = arrived.at[chunk, pl.ds(HALO, rows)]
        pltpu.make_async_copy(held, held, piece_recv.at[chunk]).wait()
        for copy in rim_copies(chunk):
            copy.start()

    def compute(chunk):
        for copy in rim_copies(chunk):
            copy.wait()

        def mask_row(row, carry):
            for r in (0, 1):
                for part in range(0, wide, 8):
                    at = slice(part, part + 8)
                    field0[row, r, at, :] = arrived[chunk, row, r, at, :] * present[row]
            return carry

        lax.fori_loop(0, padded_rows, mask_row, 0)
        sweep(field0, field1, None, present, 0)
        sweep(field1, field2, None, scaled, 1)
        sweep(field2, field3, field1, doubled, 2)
        sweep(field3, None, field2, doubled, 3)
        product = lax.dot_general(
            left_ref[...],
            rounded[:, HALO * width : (HALO + rows) * width],
            (((1,), (1,)), ((), ())),
            preferred_element_type=jnp.float32,
        )
        count_left = product.shape[0] // 2
        half = product.shape[1] // 2
        real, imaginary = product[:count_left], product[count_left:]
        swapped = pltpu.roll(imaginary, half, axis=1)
        wheres = lax.broadcasted_iota(jnp.int32, swapped.shape, 1)
        combined = real + jnp.where(wheres < half, swapped, -swapped)
        partial[pl.ds(pl.multiple_of(chunk * count_left, count_left), count_left), :] = combined

    def step_chunk(step, carry):
        @pl.when(step < chunks)
        def _():
            stage(step)

        @pl.when(step > 0)
        def _():
            compute(step - 1)

        return carry

    lax.fori_loop(0, chunks + 1, step_chunk, 0)

    share_rows = shares.shape[1]

    def rows_of(site):
        return pl.ds(pl.multiple_of(site * share_rows, share_rows), share_rows)

    def share_copy(step):
        site = lax.rem(my_site + step, sites)
        return pltpu.make_async_remote_copy(
            src_ref=partial.at[rows_of(site)],
            dst_ref=shares.at[my_site],
            send_sem=share_send.at[step],
            recv_sem=share_recv,
            device_id={"sites": site},
            device_id_type=MESH,
        )

    def total_copy(step):
        site = lax.rem(my_site + step, sites)
        return pltpu.make_async_remote_copy(
            src_ref=total.at[rows_of(my_site)],
            dst_ref=total.at[rows_of(my_site)],
            send_sem=total_send.at[step],
            recv_sem=total_recv,
            device_id={"sites": site},
            device_id_type=MESH,
        )

    def start_all(make, stop):
        def go(step, carry):
            make(step).start()
            return carry

        lax.fori_loop(1, stop, go, 0)

    def sent_all(make, stop):
        def go(step, carry):
            make(step).wait_send()
            return carry

        lax.fori_loop(1, stop, go, 0)

    start_all(share_copy, sites)
    pltpu.make_async_copy(partial.at[rows_of(my_site)], shares.at[my_site], share_recv).start()
    pltpu.make_async_copy(shares, shares, share_recv).wait()
    summed = shares[0]
    for site in range(1, sites):
        summed = summed + shares[site]
    total[rows_of(my_site), :] = summed
    start_all(total_copy, sites)
    whole = total.at[pl.ds(0, (sites - 1) * share_rows)]
    pltpu.make_async_copy(whole, whole, total_recv).wait()
    out_ref[...] = total[...]
    sent_all(share_copy, sites)
    sent_all(total_copy, sites)

    def sent_chunk(chunk, carry):
        sent_all(functools.partial(piece_copy, chunk), count)
        return carry

    lax.fori_loop(0, chunks, sent_chunk, 0)


def per_device_fused(groups, sites, right_vectors, left_vectors, vacancy):
    width_group = right_vectors.shape[1]
    count_left, rows, width = left_vectors.shape[1:]
    wide = COLS_AT_ONCE
    chunks = width_group // wide
    padded = rows + 2 * HALO
    field = pltpu.VMEM((padded, 2, wide, width), jnp.float32)
    mask = pltpu.VMEM((padded, 8, width), jnp.float32)
    sums = (chunks * count_left, 2 * MOM * wide)
    dma = pltpu.SemaphoreType.DMA
    call = pl.pallas_call(
        functools.partial(fused_kernel, groups, sites),
        out_shape=jax.ShapeDtypeStruct(sums, jnp.float32),
        in_specs=[
            pl.BlockSpec(memory_space=pl.ANY),
            pl.BlockSpec(memory_space=pltpu.VMEM),
            pl.BlockSpec(memory_space=pltpu.VMEM),
        ],
        out_specs=pl.BlockSpec(memory_space=pltpu.VMEM),
        scratch_shapes=[
            pltpu.VMEM((chunks, padded, 2, wide, width), jnp.float32),
            field, field, field, field, mask, mask, mask,
            pltpu.VMEM((2 * MOM * wide, padded * width), jnp.bfloat16),
            pltpu.VMEM(sums, jnp.float32),
            pltpu.VMEM((sites, sums[0] // sites, sums[1]), jnp.float32),
            pltpu.VMEM(sums, jnp.float32),
            dma((chunks, groups * sites)), dma((chunks,)),
            dma((chunks, 2)), dma((chunks, 2)), dma((2,)), dma((2,)),
            dma((sites,)), dma, dma((sites,)), dma,
        ],
        compiler_params=pltpu.CompilerParams(
            collective_id=0, has_side_effects=True, vmem_limit_bytes=48 * 1024 * 1024
        ),
        cost_estimate=pl.CostEstimate(flops=2 * 10**9, bytes_accessed=8 * 10**6, transcendentals=0),
    )
    summed = call(right_vectors, left_vectors.reshape(2 * count_left, rows * width), vacancy)
    summed = summed.reshape(chunks, count_left, 2, MOM, wide)
    return summed.transpose(2, 3, 1, 0, 4).reshape(2, MOM, count_left, width_group, 1)


def per_device(groups, sites, right_vectors, left_vectors, vacancy):
    columns, piece = right_vectors.shape[1], right_vectors.shape[5]
    count_left, rows, width = left_vectors.shape[1:]
    shares = (columns // COLS_AT_ONCE) * count_left
    fits = (
        piece % 128 == 0 and width % piece == 0 and right_vectors.shape[4] == 1
        and columns % COLS_AT_ONCE == 0 and rows % 2 == 0 and rows >= HALO
        and sites >= 3 and shares % (8 * sites) == 0 and count_left % 8 == 0
    )
    if fits:
        return per_device_fused(groups, sites, right_vectors, left_vectors, vacancy)
    return per_device_plain(right_vectors, left_vectors, vacancy)


def solution(mesh):
    return jax.shard_map(
        functools.partial(per_device, mesh.shape["cols"], mesh.shape["sites"]),
        mesh=mesh,
        in_specs=(
            P(None, None, None, None, ("cols", "sites"), None),
            P(None, None, "sites", None),
            P("sites", None),
        ),
        out_specs=P(None, None, None, None, "cols"),
        check_vma=False,
    )
```

```python
import functools

import jax
import jax.numpy as jnp
from jax import lax
from jax.experimental import pallas as pl
from jax.experimental.pallas import tpu as pltpu
from jax.sharding import PartitionSpec as P

MOM = 4


ONSITE_MASS = 0.3
SECOND_HOP = 0.2
BAND_SCALE = 4.5


def padded_2(cells, sides, width):
    for axis, dim in sides:
        count = lax.axis_size(axis)
        head = lax.slice_in_dim(cells, 0, width, axis=dim)
        tail = lax.slice_in_dim(cells, cells.shape[dim] - width, cells.shape[dim], axis=dim)
        cells = jnp.concatenate(
            [
                lax.ppermute(tail, axis, [(i, (i + 1) % count) for i in range(count)]),
                cells,
                lax.ppermute(head, axis, [((i + 1) % count, i) for i in range(count)]),
            ],
            axis=dim,
        )
    return cells


def column_shift(values, offset):
    row_width = values.shape[-1]
    filler = jnp.zeros(values.shape[:-1] + (abs(offset),), values.dtype)
    if offset > 0:
        return jnp.concatenate([values[..., offset:], filler], axis=-1)
    return jnp.concatenate([filler, values[..., : row_width + offset]], axis=-1)


def rotate_phase(values):
    return jnp.stack([-values[1], values[0]])


def sign_table(row_count, row_width):
    rows_index = lax.broadcasted_iota(jnp.int32, (row_count, row_width), 0)
    cols_index = lax.broadcasted_iota(jnp.int32, (row_count, row_width), 1)
    return (1 - 2 * ((rows_index + cols_index) % 2)).astype(jnp.float32)


def haldane(padded, parity_sign):
    centre = padded[:, :, 1:-1, :]
    upper_row = padded[:, :, 2:, :]
    lower_row = padded[:, :, :-2, :]
    vertical = jnp.where(parity_sign > 0, upper_row, lower_row)
    nearest = column_shift(centre, 1) + column_shift(centre, -1) + vertical
    second = (
        column_shift(centre, 2)
        - column_shift(centre, -2)
        + column_shift(upper_row, -1)
        - column_shift(lower_row, 1)
        + column_shift(lower_row, -1)
        - column_shift(upper_row, 1)
    )
    return (
        ONSITE_MASS * parity_sign * centre
        + nearest
        + SECOND_HOP * parity_sign * rotate_phase(second)
    )


def velocity(padded, parity_sign):
    centre = padded[:, :, 1:-1, :]
    upper_row = padded[:, :, 2:, :]
    lower_row = padded[:, :, :-2, :]
    along_x = column_shift(centre, 1) - column_shift(centre, -1)
    farther = column_shift(centre, 2) + column_shift(centre, -2)
    diagonal = (
        column_shift(upper_row, 1)
        + column_shift(upper_row, -1)
        + column_shift(lower_row, 1)
        + column_shift(lower_row, -1)
    )
    return rotate_phase(along_x) - SECOND_HOP * parity_sign * (2.0 * farther - diagonal)


def with_rims(values):
    return padded_2(values, (("sites", 2),), 1)


def per_device_plain(right_vectors, left_vectors, vacancy):
    layout = right_vectors.shape
    pieces = right_vectors.reshape(layout[0], layout[1], layout[2], layout[3], layout[5])
    slab_field = lax.all_to_all(
        lax.all_to_all(pieces, "cols", split_axis=2, concat_axis=2, tiled=True),
        "sites",
        split_axis=3,
        concat_axis=3,
        tiled=True,
    )
    row_count = left_vectors.shape[2]
    row_width = left_vectors.shape[3]
    count_left = left_vectors.shape[1]
    group_width = layout[1]
    site_count = row_count * row_width
    present = vacancy.astype(jnp.float32)
    current = slab_field.reshape(2, group_width, row_count, row_width) * present
    parity_sign = sign_table(row_count, row_width)
    latest = velocity(with_rims(current), parity_sign) * present
    previous = latest
    moment_list = [latest]
    for degree in range(1, MOM):
        applied = haldane(with_rims(latest), parity_sign) * present / BAND_SCALE
        following = applied if degree == 1 else 2.0 * applied - previous
        previous, latest = (latest, following)
        moment_list.append(latest)
    left_matrix = left_vectors.reshape(2 * count_left, site_count)
    summed_list = []
    for moment in moment_list:
        rounded = moment.astype(jnp.bfloat16).reshape(2 * group_width, site_count)
        product = lax.dot_general(
            left_matrix, rounded, (((1,), (1,)), ((), ())), preferred_element_type=jnp.float32
        ).reshape(2, count_left, 2, group_width)
        combined = jnp.stack(
            [product[0, :, 0] + product[1, :, 1], product[0, :, 1] - product[1, :, 0]]
        )
        summed_list.append(lax.psum(combined, "sites"))
    summed = jnp.stack(summed_list, axis=1)
    return summed[..., None]


MESH = pl.DeviceIdType.MESH
HALO = MOM
COLS_AT_ONCE = 16


def fused_kernel(
    groups, sites, right_ref, left_ref, vacancy_ref, out_ref,
    arrived, field0, field1, field2, field3, present, scaled, doubled, rounded,
    partial, shares, total,
    piece_send, piece_recv, rim_send, rim_recv, mask_send, mask_recv,
    share_send, share_recv, total_send, total_recv,
):
    chunks, padded_rows, _, wide, width = arrived.shape
    rows = padded_rows - 2 * HALO
    piece = right_ref.shape[5]
    per_row = width // piece
    count = groups * sites
    my_group, my_site = lax.axis_index("cols"), lax.axis_index("sites")
    mine = my_group * sites + my_site
    above, below = lax.rem(my_site + 1, sites), lax.rem(my_site + sites - 1, sites)

    barrier = pltpu.get_barrier_semaphore()

    def greet(step, carry):
        other = lax.rem(mine + step, count)
        pl.semaphore_signal(
            barrier, inc=1, device_id={"cols": other // sites, "sites": lax.rem(other, sites)}, device_id_type=MESH
        )
        return carry

    lax.fori_loop(1, count, greet, 0)

    lane = lax.broadcasted_iota(jnp.int32, (8, width), 1)
    odd_lane = lax.rem(lane, 2) == 1

    for row in range(rows):
        present[HALO + row] = jnp.broadcast_to(vacancy_ref[row : row + 1, :].astype(jnp.float32), (8, width))

    pl.semaphore_wait(barrier, count - 1)

    def landing(chunk, run):
        return arrived.at[
            chunk, HALO + run // per_row, :, :, pl.ds(pl.multiple_of(lax.rem(run, per_row) * piece, piece), piece)
        ]

    def piece_of(chunk, group, site):
        return right_ref.at[:, pl.ds(pl.multiple_of(chunk * wide, wide), wide), group, site, 0, :]

    def piece_copy(chunk, step):
        other = lax.rem(mine + step, count)
        group, site = other // sites, lax.rem(other, sites)
        return pltpu.make_async_remote_copy(
            src_ref=piece_of(chunk, group, site),
            dst_ref=landing(chunk, mine),
            send_sem=piece_send.at[chunk, step],
            recv_sem=piece_recv.at[chunk],
            device_id={"cols": group, "sites": site},
            device_id_type=MESH,
        )

    def rim_copy(source, send_sem, recv_sem, up):
        first = rows if up else HALO
        landing_row = 0 if up else rows + HALO
        return pltpu.make_async_remote_copy(
            src_ref=source.at[pl.ds(first, HALO)],
            dst_ref=source.at[pl.ds(landing_row, HALO)],
            send_sem=send_sem,
            recv_sem=recv_sem,
            device_id={"sites": above if up else below},
            device_id_type=MESH,
        )

    def mask_copies():
        return [rim_copy(present, mask_send.at[i], mask_recv.at[i], up) for i, up in enumerate((True, False))]

    def rim_copies(chunk):
        return [
            rim_copy(arrived.at[chunk], rim_send.at[chunk, i], rim_recv.at[chunk, i], up)
            for i, up in enumerate((True, False))
        ]

    for copy in mask_copies():
        copy.start()

    def send_chunk(chunk, carry):
        def send(step, inner):
            piece_copy(chunk, step).start()
            return inner

        lax.fori_loop(1, count, send, 0)
        pltpu.make_async_copy(piece_of(chunk, my_group, my_site), landing(chunk, mine), piece_recv.at[chunk]).start()
        return carry

    lax.fori_loop(0, min(2, chunks), send_chunk, 0)

    for copy in mask_copies():
        copy.wait()

    def scale_masks(row, carry):
        held = present[row]
        scaled[row] = held * (1.0 / BAND_SCALE)
        doubled[row] = held * (2.0 / BAND_SCALE)
        return carry

    lax.fori_loop(0, padded_rows, scale_masks, 0)

    def shift(values, offset):
        turned = pltpu.roll(values, width - 1 if offset > 0 else 1, axis=1)
        return jnp.where(lane == (width - 1 if offset > 0 else 0), 0.0, turned)

    def signed(values, odd_row):
        return jnp.where(odd_lane != odd_row, -values, values)

    def sweep(source, target, earlier, mask, degree):
        first = degree + 1

        def one_row(row, odd_row):
            halves = [[], []]
            for part in range(0, wide, 8):
                at = slice(part, part + 8)
                centre = [source[row, r, at, :] for r in (0, 1)]
                upper = [source[row + 1, r, at, :] for r in (0, 1)]
                lower = [source[row - 1, r, at, :] for r in (0, 1)]
                right = [shift(c, 1) for c in centre]
                left = [shift(c, -1) for c in centre]
                both = [u + l for u, l in zip(upper, lower)]
                if degree == 0:
                    far = [shift(2.0 * a - s, 1) + shift(2.0 * b - s, -1) for a, b, s in zip(right, left, both)]
                    near = [a - b for a, b in zip(right, left)]
                    applied = [
                        -near[1] - signed(SECOND_HOP * far[0], odd_row),
                        near[0] - signed(SECOND_HOP * far[1], odd_row),
                    ]
                else:
                    far = [shift(a - s, 1) - shift(b - s, -1) for a, b, s in zip(right, left, both)]
                    phase = [-far[1], far[0]]
                    applied = [
                        signed(ONSITE_MASS * centre[r] + SECOND_HOP * phase[r], odd_row)
                        + (right[r] + left[r])
                        + jnp.where(odd_lane != odd_row, lower[r], upper[r])
                        for r in (0, 1)
                    ]
                factor = mask[row]
                for r in (0, 1):
                    result = applied[r] * factor
                    if earlier is not None:
                        result = result - earlier[row, r, at, :]
                    if target is not None:
                        target[row, r, at, :] = result
                    halves[r].append(result)
            lanes = pl.ds(pl.multiple_of(row * width, width), width)
            for r in (0, 1):
                base = (r * MOM + degree) * wide
                rounded[base : base + wide, lanes] = jnp.concatenate(halves[r], axis=0).astype(jnp.bfloat16)

        def pair(step, carry):
            one_row(first + 2 * step, first % 2 == 1)
            one_row(first + 2 * step + 1, first % 2 == 0)
            return carry

        lax.fori_loop(0, (padded_rows - 2 * first) // 2, pair, 0)

    def stage(chunk):
        held = arrived.at[chunk, pl.ds(HALO, rows)]
        pltpu.make_async_copy(held, held, piece_recv.at[chunk]).wait()
        for copy in rim_copies(chunk):
            copy.start()

        @pl.when(chunk + 2 < chunks)
        def _():
            send_chunk(chunk + 2, 0)

    def compute(chunk):
        for copy in rim_copies(chunk):
            copy.wait()

        def mask_row(row, carry):
            for r in (0, 1):
                for part in range(0, wide, 8):
                    at = slice(part, part + 8)
                    field0[row, r, at, :] = arrived[chunk, row, r, at, :] * present[row]
            return carry

        lax.fori_loop(0, padded_rows, mask_row, 0)
        sweep(field0, field1, None, present, 0)
        sweep(field1, field2, None, scaled, 1)
        sweep(field2, field3, field1, doubled, 2)
        sweep(field3, None, field2, doubled, 3)
        product = lax.dot_general(
            left_ref[...],
            rounded[:, HALO * width : (HALO + rows) * width],
            (((1,), (1,)), ((), ())),
            preferred_element_type=jnp.float32,
        )
        count_left = product.shape[0] // 2
        half = product.shape[1] // 2
        real, imaginary = product[:count_left], product[count_left:]
        swapped = pltpu.roll(imaginary, half, axis=1)
        wheres = lax.broadcasted_iota(jnp.int32, swapped.shape, 1)
        combined = real + jnp.where(wheres < half, swapped, -swapped)
        partial[pl.ds(pl.multiple_of(chunk * count_left, count_left), count_left), :] = combined

    def step_chunk(step, carry):
        @pl.when(step < chunks)
        def _():
            stage(step)

        @pl.when(step > 0)
        def _():
            compute(step - 1)

        return carry

    lax.fori_loop(0, chunks + 1, step_chunk, 0)

    share_rows = shares.shape[1]

    def rows_of(site):
        return pl.ds(pl.multiple_of(site * share_rows, share_rows), share_rows)

    def share_copy(step):
        site = lax.rem(my_site + step, sites)
        return pltpu.make_async_remote_copy(
            src_ref=partial.at[rows_of(site)],
            dst_ref=shares.at[my_site],
            send_sem=share_send.at[step],
            recv_sem=share_recv,
            device_id={"sites": site},
            device_id_type=MESH,
        )

    def total_copy(step):
        site = lax.rem(my_site + step, sites)
        return pltpu.make_async_remote_copy(
            src_ref=total.at[rows_of(my_site)],
            dst_ref=total.at[rows_of(my_site)],
            send_sem=total_send.at[step],
            recv_sem=total_recv,
            device_id={"sites": site},
            device_id_type=MESH,
        )

    def start_all(make, stop):
        def go(step, carry):
            make(step).start()
            return carry

        lax.fori_loop(1, stop, go, 0)

    def sent_all(make, stop):
        def go(step, carry):
            make(step).wait_send()
            return carry

        lax.fori_loop(1, stop, go, 0)

    start_all(share_copy, sites)
    pltpu.make_async_copy(partial.at[rows_of(my_site)], shares.at[my_site], share_recv).start()
    pltpu.make_async_copy(shares, shares, share_recv).wait()
    summed = shares[0]
    for site in range(1, sites):
        summed = summed + shares[site]
    total[rows_of(my_site), :] = summed
    start_all(total_copy, sites)
    whole = total.at[pl.ds(0, (sites - 1) * share_rows)]
    pltpu.make_async_copy(whole, whole, total_recv).wait()
    out_ref[...] = total[...]
    sent_all(share_copy, sites)
    sent_all(total_copy, sites)

    def sent_chunk(chunk, carry):
        sent_all(functools.partial(piece_copy, chunk), count)
        return carry

    lax.fori_loop(0, chunks, sent_chunk, 0)


def per_device_fused(groups, sites, right_vectors, left_vectors, vacancy):
    width_group = right_vectors.shape[1]
    count_left, rows, width = left_vectors.shape[1:]
    wide = COLS_AT_ONCE
    chunks = width_group // wide
    padded = rows + 2 * HALO
    field = pltpu.VMEM((padded, 2, wide, width), jnp.float32)
    mask = pltpu.VMEM((padded, 8, width), jnp.float32)
    sums = (chunks * count_left, 2 * MOM * wide)
    dma = pltpu.SemaphoreType.DMA
    call = pl.pallas_call(
        functools.partial(fused_kernel, groups, sites),
        out_shape=jax.ShapeDtypeStruct(sums, jnp.float32),
        in_specs=[
            pl.BlockSpec(memory_space=pl.ANY),
            pl.BlockSpec(memory_space=pltpu.VMEM),
            pl.BlockSpec(memory_space=pltpu.VMEM),
        ],
        out_specs=pl.BlockSpec(memory_space=pltpu.VMEM),
        scratch_shapes=[
            pltpu.VMEM((chunks, padded, 2, wide, width), jnp.float32),
            field, field, field, field, mask, mask, mask,
            pltpu.VMEM((2 * MOM * wide, padded * width), jnp.bfloat16),
            pltpu.VMEM(sums, jnp.float32),
            pltpu.VMEM((sites, sums[0] // sites, sums[1]), jnp.float32),
            pltpu.VMEM(sums, jnp.float32),
            dma((chunks, groups * sites)), dma((chunks,)),
            dma((chunks, 2)), dma((chunks, 2)), dma((2,)), dma((2,)),
            dma((sites,)), dma, dma((sites,)), dma,
        ],
        compiler_params=pltpu.CompilerParams(
            collective_id=0, has_side_effects=True, vmem_limit_bytes=48 * 1024 * 1024
        ),
        cost_estimate=pl.CostEstimate(flops=2 * 10**9, bytes_accessed=8 * 10**6, transcendentals=0),
    )
    summed = call(right_vectors, left_vectors.reshape(2 * count_left, rows * width), vacancy)
    summed = summed.reshape(chunks, count_left, 2, MOM, wide)
    return summed.transpose(2, 3, 1, 0, 4).reshape(2, MOM, count_left, width_group, 1)


def per_device(groups, sites, right_vectors, left_vectors, vacancy):
    columns, piece = right_vectors.shape[1], right_vectors.shape[5]
    count_left, rows, width = left_vectors.shape[1:]
    shares = (columns // COLS_AT_ONCE) * count_left
    fits = (
        piece % 128 == 0 and width % piece == 0 and right_vectors.shape[4] == 1
        and columns % COLS_AT_ONCE == 0 and rows % 2 == 0 and rows >= HALO
        and sites >= 3 and shares % (8 * sites) == 0 and count_left % 8 == 0
    )
    if fits:
        return per_device_fused(groups, sites, right_vectors, left_vectors, vacancy)
    return per_device_plain(right_vectors, left_vectors, vacancy)


def solution(mesh):
    return jax.shard_map(
        functools.partial(per_device, mesh.shape["cols"], mesh.shape["sites"]),
        mesh=mesh,
        in_specs=(
            P(None, None, None, None, ("cols", "sites"), None),
            P(None, None, "sites", None),
            P("sites", None),
        ),
        out_specs=P(None, None, None, None, "cols"),
        check_vma=False,
    )
```

```python
import functools

import jax
import jax.numpy as jnp
from jax import lax
from jax.experimental import pallas as pl
from jax.experimental.pallas import tpu as pltpu
from jax.sharding import PartitionSpec as P

MOM = 4


ONSITE_MASS = 0.3
SECOND_HOP = 0.2
BAND_SCALE = 4.5


def padded_2(cells, sides, width):
    for axis, dim in sides:
        count = lax.axis_size(axis)
        head = lax.slice_in_dim(cells, 0, width, axis=dim)
        tail = lax.slice_in_dim(cells, cells.shape[dim] - width, cells.shape[dim], axis=dim)
        cells = jnp.concatenate(
            [
                lax.ppermute(tail, axis, [(i, (i + 1) % count) for i in range(count)]),
                cells,
                lax.ppermute(head, axis, [((i + 1) % count, i) for i in range(count)]),
            ],
            axis=dim,
        )
    return cells


def column_shift(values, offset):
    row_width = values.shape[-1]
    filler = jnp.zeros(values.shape[:-1] + (abs(offset),), values.dtype)
    if offset > 0:
        return jnp.concatenate([values[..., offset:], filler], axis=-1)
    return jnp.concatenate([filler, values[..., : row_width + offset]], axis=-1)


def rotate_phase(values):
    return jnp.stack([-values[1], values[0]])


def sign_table(row_count, row_width):
    rows_index = lax.broadcasted_iota(jnp.int32, (row_count, row_width), 0)
    cols_index = lax.broadcasted_iota(jnp.int32, (row_count, row_width), 1)
    return (1 - 2 * ((rows_index + cols_index) % 2)).astype(jnp.float32)


def haldane(padded, parity_sign):
    centre = padded[:, :, 1:-1, :]
    upper_row = padded[:, :, 2:, :]
    lower_row = padded[:, :, :-2, :]
    vertical = jnp.where(parity_sign > 0, upper_row, lower_row)
    nearest = column_shift(centre, 1) + column_shift(centre, -1) + vertical
    second = (
        column_shift(centre, 2)
        - column_shift(centre, -2)
        + column_shift(upper_row, -1)
        - column_shift(lower_row, 1)
        + column_shift(lower_row, -1)
        - column_shift(upper_row, 1)
    )
    return (
        ONSITE_MASS * parity_sign * centre
        + nearest
        + SECOND_HOP * parity_sign * rotate_phase(second)
    )


def velocity(padded, parity_sign):
    centre = padded[:, :, 1:-1, :]
    upper_row = padded[:, :, 2:, :]
    lower_row = padded[:, :, :-2, :]
    along_x = column_shift(centre, 1) - column_shift(centre, -1)
    farther = column_shift(centre, 2) + column_shift(centre, -2)
    diagonal = (
        column_shift(upper_row, 1)
        + column_shift(upper_row, -1)
        + column_shift(lower_row, 1)
        + column_shift(lower_row, -1)
    )
    return rotate_phase(along_x) - SECOND_HOP * parity_sign * (2.0 * farther - diagonal)


def with_rims(values):
    return padded_2(values, (("sites", 2),), 1)


def per_device_plain(right_vectors, left_vectors, vacancy):
    layout = right_vectors.shape
    pieces = right_vectors.reshape(layout[0], layout[1], layout[2], layout[3], layout[5])
    slab_field = lax.all_to_all(
        lax.all_to_all(pieces, "cols", split_axis=2, concat_axis=2, tiled=True),
        "sites",
        split_axis=3,
        concat_axis=3,
        tiled=True,
    )
    row_count = left_vectors.shape[2]
    row_width = left_vectors.shape[3]
    count_left = left_vectors.shape[1]
    group_width = layout[1]
    site_count = row_count * row_width
    present = vacancy.astype(jnp.float32)
    current = slab_field.reshape(2, group_width, row_count, row_width) * present
    parity_sign = sign_table(row_count, row_width)
    latest = velocity(with_rims(current), parity_sign) * present
    previous = latest
    moment_list = [latest]
    for degree in range(1, MOM):
        applied = haldane(with_rims(latest), parity_sign) * present / BAND_SCALE
        following = applied if degree == 1 else 2.0 * applied - previous
        previous, latest = (latest, following)
        moment_list.append(latest)
    left_matrix = left_vectors.reshape(2 * count_left, site_count)
    summed_list = []
    for moment in moment_list:
        rounded = moment.astype(jnp.bfloat16).reshape(2 * group_width, site_count)
        product = lax.dot_general(
            left_matrix, rounded, (((1,), (1,)), ((), ())), preferred_element_type=jnp.float32
        ).reshape(2, count_left, 2, group_width)
        combined = jnp.stack(
            [product[0, :, 0] + product[1, :, 1], product[0, :, 1] - product[1, :, 0]]
        )
        summed_list.append(lax.psum(combined, "sites"))
    summed = jnp.stack(summed_list, axis=1)
    return summed[..., None]


MESH = pl.DeviceIdType.MESH
HALO = MOM
COLS_AT_ONCE = 16


def fused_kernel(
    groups, sites, right_ref, left_ref, vacancy_ref, out_ref,
    arrived, field0, field1, field2, field3, present, scaled, doubled, rounded,
    partial, shares, total,
    piece_send, piece_recv, rim_send, rim_recv, mask_send, mask_recv,
    share_send, share_recv, total_send, total_recv,
):
    chunks, padded_rows, _, wide, width = arrived.shape
    rows = padded_rows - 2 * HALO
    piece = right_ref.shape[5]
    per_row = width // piece
    count = groups * sites
    my_group, my_site = lax.axis_index("cols"), lax.axis_index("sites")
    mine = my_group * sites + my_site
    above, below = lax.rem(my_site + 1, sites), lax.rem(my_site + sites - 1, sites)

    barrier = pltpu.get_barrier_semaphore()

    def greet(step, carry):
        other = lax.rem(mine + step, count)
        pl.semaphore_signal(
            barrier, inc=1, device_id={"cols": other // sites, "sites": lax.rem(other, sites)}, device_id_type=MESH
        )
        return carry

    lax.fori_loop(1, count, greet, 0)

    lane = lax.broadcasted_iota(jnp.int32, (8, width), 1)
    odd_lane = lax.rem(lane, 2) == 1

    for row in range(rows):
        present[HALO + row] = jnp.broadcast_to(vacancy_ref[row : row + 1, :].astype(jnp.float32), (8, width))

    pl.semaphore_wait(barrier, count - 1)

    def landing(chunk, run):
        return arrived.at[
            chunk, HALO + run // per_row, :, :, pl.ds(pl.multiple_of(lax.rem(run, per_row) * piece, piece), piece)
        ]

    def piece_of(chunk, group, site):
        return right_ref.at[:, pl.ds(pl.multiple_of(chunk * wide, wide), wide), group, site, 0, :]

    def piece_copy(chunk, step):
        turn = lax.rem(step, 2) * (sites // 2) + step // (2 * groups)
        group = lax.rem(my_group + lax.rem(step // 2, groups), groups)
        site = lax.rem(my_site + turn, sites)
        return pltpu.make_async_remote_copy(
            src_ref=piece_of(chunk, group, site),
            dst_ref=landing(chunk, mine),
            send_sem=piece_send.at[chunk, step],
            recv_sem=piece_recv.at[chunk],
            device_id={"cols": group, "sites": site},
            device_id_type=MESH,
        )

    def rim_copy(source, send_sem, recv_sem, up):
        first = rows if up else HALO
        landing_row = 0 if up else rows + HALO
        return pltpu.make_async_remote_copy(
            src_ref=source.at[pl.ds(first, HALO)],
            dst_ref=source.at[pl.ds(landing_row, HALO)],
            send_sem=send_sem,
            recv_sem=recv_sem,
            device_id={"sites": above if up else below},
            device_id_type=MESH,
        )

    def mask_copies():
        return [rim_copy(present, mask_send.at[i], mask_recv.at[i], up) for i, up in enumerate((True, False))]

    def rim_copies(chunk):
        return [
            rim_copy(arrived.at[chunk], rim_send.at[chunk, i], rim_recv.at[chunk, i], up)
            for i, up in enumerate((True, False))
        ]

    for copy in mask_copies():
        copy.start()

    def send_chunk(chunk, carry):
        def send(step, inner):
            piece_copy(chunk, step).start()
            return inner

        lax.fori_loop(1, count, send, 0)
        pltpu.make_async_copy(piece_of(chunk, my_group, my_site), landing(chunk, mine), piece_recv.at[chunk]).start()
        return carry

    lax.fori_loop(0, min(2, chunks), send_chunk, 0)

    for copy in mask_copies():
        copy.wait()

    def scale_masks(row, carry):
        held = present[row]
        scaled[row] = held * (1.0 / BAND_SCALE)
        doubled[row] = held * (2.0 / BAND_SCALE)
        return carry

    lax.fori_loop(0, padded_rows, scale_masks, 0)

    def shift(values, offset):
        turned = pltpu.roll(values, width - 1 if offset > 0 else 1, axis=1)
        return jnp.where(lane == (width - 1 if offset > 0 else 0), 0.0, turned)

    def signed(values, odd_row):
        return jnp.where(odd_lane != odd_row, -values, values)

    def sweep(source, target, earlier, mask, degree):
        first = degree + 1

        def one_row(row, odd_row):
            halves = [[], []]
            for part in range(0, wide, 8):
                at = slice(part, part + 8)
                centre = [source[row, r, at, :] for r in (0, 1)]
                upper = [source[row + 1, r, at, :] for r in (0, 1)]
                lower = [source[row - 1, r, at, :] for r in (0, 1)]
                right = [shift(c, 1) for c in centre]
                left = [shift(c, -1) for c in centre]
                both = [u + l for u, l in zip(upper, lower)]
                if degree == 0:
                    far = [shift(2.0 * a - s, 1) + shift(2.0 * b - s, -1) for a, b, s in zip(right, left, both)]
                    near = [a - b for a, b in zip(right, left)]
                    applied = [
                        -near[1] - signed(SECOND_HOP * far[0], odd_row),
                        near[0] - signed(SECOND_HOP * far[1], odd_row),
                    ]
                else:
                    far = [shift(a - s, 1) - shift(b - s, -1) for a, b, s in zip(right, left, both)]
                    phase = [-far[1], far[0]]
                    applied = [
                        signed(ONSITE_MASS * centre[r] + SECOND_HOP * phase[r], odd_row)
                        + (right[r] + left[r])
                        + jnp.where(odd_lane != odd_row, lower[r], upper[r])
                        for r in (0, 1)
                    ]
                factor = mask[row]
                for r in (0, 1):
                    result = applied[r] * factor
                    if earlier is not None:
                        result = result - earlier[row, r, at, :]
                    if target is not None:
                        target[row, r, at, :] = result
                    halves[r].append(result)
            lanes = pl.ds(pl.multiple_of(row * width, width), width)
            for r in (0, 1):
                base = (r * MOM + degree) * wide
                rounded[base : base + wide, lanes] = jnp.concatenate(halves[r], axis=0).astype(jnp.bfloat16)

        def pair(step, carry):
            one_row(first + 2 * step, first % 2 == 1)
            one_row(first + 2 * step + 1, first % 2 == 0)
            return carry

        lax.fori_loop(0, (padded_rows - 2 * first) // 2, pair, 0)

    def stage(chunk):
        held = arrived.at[chunk, pl.ds(HALO, rows)]
        pltpu.make_async_copy(held, held, piece_recv.at[chunk]).wait()
        for copy in rim_copies(chunk):
            copy.start()

        @pl.when(chunk + 2 < chunks)
        def _():
            send_chunk(chunk + 2, 0)

    def compute(chunk):
        for copy in rim_copies(chunk):
            copy.wait()

        def mask_row(row, carry):
            for r in (0, 1):
                for part in range(0, wide, 8):
                    at = slice(part, part + 8)
                    field0[row, r, at, :] = arrived[chunk, row, r, at, :] * present[row]
            return carry

        lax.fori_loop(0, padded_rows, mask_row, 0)
        sweep(field0, field1, None, present, 0)
        sweep(field1, field2, None, scaled, 1)
        sweep(field2, field3, field1, doubled, 2)
        sweep(field3, None, field2, doubled, 3)
        product = lax.dot_general(
            left_ref[...],
            rounded[:, HALO * width : (HALO + rows) * width],
            (((1,), (1,)), ((), ())),
            preferred_element_type=jnp.float32,
        )
        count_left = product.shape[0] // 2
        half = product.shape[1] // 2
        real, imaginary = product[:count_left], product[count_left:]
        swapped = pltpu.roll(imaginary, half, axis=1)
        wheres = lax.broadcasted_iota(jnp.int32, swapped.shape, 1)
        combined = real + jnp.where(wheres < half, swapped, -swapped)
        partial[pl.ds(pl.multiple_of(chunk * count_left, count_left), count_left), :] = combined

    def step_chunk(step, carry):
        @pl.when(step < chunks)
        def _():
            stage(step)

        @pl.when(step > 0)
        def _():
            compute(step - 1)

        return carry

    lax.fori_loop(0, chunks + 1, step_chunk, 0)

    share_rows = shares.shape[1]

    def rows_of(site):
        return pl.ds(pl.multiple_of(site * share_rows, share_rows), share_rows)

    def share_copy(step):
        site = lax.rem(my_site + step, sites)
        return pltpu.make_async_remote_copy(
            src_ref=partial.at[rows_of(site)],
            dst_ref=shares.at[my_site],
            send_sem=share_send.at[step],
            recv_sem=share_recv,
            device_id={"sites": site},
            device_id_type=MESH,
        )

    def total_copy(step):
        site = lax.rem(my_site + step, sites)
        return pltpu.make_async_remote_copy(
            src_ref=total.at[rows_of(my_site)],
            dst_ref=total.at[rows_of(my_site)],
            send_sem=total_send.at[step],
            recv_sem=total_recv,
            device_id={"sites": site},
            device_id_type=MESH,
        )

    def start_all(make, stop):
        def go(step, carry):
            make(step).start()
            return carry

        lax.fori_loop(1, stop, go, 0)

    def sent_all(make, stop):
        def go(step, carry):
            make(step).wait_send()
            return carry

        lax.fori_loop(1, stop, go, 0)

    start_all(share_copy, sites)
    pltpu.make_async_copy(partial.at[rows_of(my_site)], shares.at[my_site], share_recv).start()
    pltpu.make_async_copy(shares, shares, share_recv).wait()
    summed = shares[0]
    for site in range(1, sites):
        summed = summed + shares[site]
    total[rows_of(my_site), :] = summed
    start_all(total_copy, sites)
    whole = total.at[pl.ds(0, (sites - 1) * share_rows)]
    pltpu.make_async_copy(whole, whole, total_recv).wait()
    out_ref[...] = total[...]
    sent_all(share_copy, sites)
    sent_all(total_copy, sites)

    def sent_chunk(chunk, carry):
        sent_all(functools.partial(piece_copy, chunk), count)
        return carry

    lax.fori_loop(0, chunks, sent_chunk, 0)


def per_device_fused(groups, sites, right_vectors, left_vectors, vacancy):
    width_group = right_vectors.shape[1]
    count_left, rows, width = left_vectors.shape[1:]
    wide = COLS_AT_ONCE
    chunks = width_group // wide
    padded = rows + 2 * HALO
    field = pltpu.VMEM((padded, 2, wide, width), jnp.float32)
    mask = pltpu.VMEM((padded, 8, width), jnp.float32)
    sums = (chunks * count_left, 2 * MOM * wide)
    dma = pltpu.SemaphoreType.DMA
    call = pl.pallas_call(
        functools.partial(fused_kernel, groups, sites),
        out_shape=jax.ShapeDtypeStruct(sums, jnp.float32),
        in_specs=[
            pl.BlockSpec(memory_space=pl.ANY),
            pl.BlockSpec(memory_space=pltpu.VMEM),
            pl.BlockSpec(memory_space=pltpu.VMEM),
        ],
        out_specs=pl.BlockSpec(memory_space=pltpu.VMEM),
        scratch_shapes=[
            pltpu.VMEM((chunks, padded, 2, wide, width), jnp.float32),
            field, field, field, field, mask, mask, mask,
            pltpu.VMEM((2 * MOM * wide, padded * width), jnp.bfloat16),
            pltpu.VMEM(sums, jnp.float32),
            pltpu.VMEM((sites, sums[0] // sites, sums[1]), jnp.float32),
            pltpu.VMEM(sums, jnp.float32),
            dma((chunks, groups * sites)), dma((chunks,)),
            dma((chunks, 2)), dma((chunks, 2)), dma((2,)), dma((2,)),
            dma((sites,)), dma, dma((sites,)), dma,
        ],
        compiler_params=pltpu.CompilerParams(
            collective_id=0, has_side_effects=True, vmem_limit_bytes=48 * 1024 * 1024
        ),
        cost_estimate=pl.CostEstimate(flops=2 * 10**9, bytes_accessed=8 * 10**6, transcendentals=0),
    )
    summed = call(right_vectors, left_vectors.reshape(2 * count_left, rows * width), vacancy)
    summed = summed.reshape(chunks, count_left, 2, MOM, wide)
    return summed.transpose(2, 3, 1, 0, 4).reshape(2, MOM, count_left, width_group, 1)


def per_device(groups, sites, right_vectors, left_vectors, vacancy):
    columns, piece = right_vectors.shape[1], right_vectors.shape[5]
    count_left, rows, width = left_vectors.shape[1:]
    shares = (columns // COLS_AT_ONCE) * count_left
    fits = (
        piece % 128 == 0 and width % piece == 0 and right_vectors.shape[4] == 1
        and columns % COLS_AT_ONCE == 0 and rows % 2 == 0 and rows >= HALO
        and sites >= 4 and sites % 2 == 0 and shares % (8 * sites) == 0 and count_left % 8 == 0
    )
    if fits:
        return per_device_fused(groups, sites, right_vectors, left_vectors, vacancy)
    return per_device_plain(right_vectors, left_vectors, vacancy)


def solution(mesh):
    return jax.shard_map(
        functools.partial(per_device, mesh.shape["cols"], mesh.shape["sites"]),
        mesh=mesh,
        in_specs=(
            P(None, None, None, None, ("cols", "sites"), None),
            P(None, None, "sites", None),
            P("sites", None),
        ),
        out_specs=P(None, None, None, None, "cols"),
        check_vma=False,
    )
```

```python
import functools

import jax
import jax.numpy as jnp
from jax import lax
from jax.experimental import pallas as pl
from jax.experimental.pallas import tpu as pltpu
from jax.sharding import PartitionSpec as P

MOM = 4


ONSITE_MASS = 0.3
SECOND_HOP = 0.2
BAND_SCALE = 4.5


def padded_2(cells, sides, width):
    for axis, dim in sides:
        count = lax.axis_size(axis)
        head = lax.slice_in_dim(cells, 0, width, axis=dim)
        tail = lax.slice_in_dim(cells, cells.shape[dim] - width, cells.shape[dim], axis=dim)
        cells = jnp.concatenate(
            [
                lax.ppermute(tail, axis, [(i, (i + 1) % count) for i in range(count)]),
                cells,
                lax.ppermute(head, axis, [((i + 1) % count, i) for i in range(count)]),
            ],
            axis=dim,
        )
    return cells


def column_shift(values, offset):
    row_width = values.shape[-1]
    filler = jnp.zeros(values.shape[:-1] + (abs(offset),), values.dtype)
    if offset > 0:
        return jnp.concatenate([values[..., offset:], filler], axis=-1)
    return jnp.concatenate([filler, values[..., : row_width + offset]], axis=-1)


def rotate_phase(values):
    return jnp.stack([-values[1], values[0]])


def sign_table(row_count, row_width):
    rows_index = lax.broadcasted_iota(jnp.int32, (row_count, row_width), 0)
    cols_index = lax.broadcasted_iota(jnp.int32, (row_count, row_width), 1)
    return (1 - 2 * ((rows_index + cols_index) % 2)).astype(jnp.float32)


def haldane(padded, parity_sign):
    centre = padded[:, :, 1:-1, :]
    upper_row = padded[:, :, 2:, :]
    lower_row = padded[:, :, :-2, :]
    vertical = jnp.where(parity_sign > 0, upper_row, lower_row)
    nearest = column_shift(centre, 1) + column_shift(centre, -1) + vertical
    second = (
        column_shift(centre, 2)
        - column_shift(centre, -2)
        + column_shift(upper_row, -1)
        - column_shift(lower_row, 1)
        + column_shift(lower_row, -1)
        - column_shift(upper_row, 1)
    )
    return (
        ONSITE_MASS * parity_sign * centre
        + nearest
        + SECOND_HOP * parity_sign * rotate_phase(second)
    )


def velocity(padded, parity_sign):
    centre = padded[:, :, 1:-1, :]
    upper_row = padded[:, :, 2:, :]
    lower_row = padded[:, :, :-2, :]
    along_x = column_shift(centre, 1) - column_shift(centre, -1)
    farther = column_shift(centre, 2) + column_shift(centre, -2)
    diagonal = (
        column_shift(upper_row, 1)
        + column_shift(upper_row, -1)
        + column_shift(lower_row, 1)
        + column_shift(lower_row, -1)
    )
    return rotate_phase(along_x) - SECOND_HOP * parity_sign * (2.0 * farther - diagonal)


def with_rims(values):
    return padded_2(values, (("sites", 2),), 1)


def per_device_plain(right_vectors, left_vectors, vacancy):
    layout = right_vectors.shape
    pieces = right_vectors.reshape(layout[0], layout[1], layout[2], layout[3], layout[5])
    slab_field = lax.all_to_all(
        lax.all_to_all(pieces, "cols", split_axis=2, concat_axis=2, tiled=True),
        "sites",
        split_axis=3,
        concat_axis=3,
        tiled=True,
    )
    row_count = left_vectors.shape[2]
    row_width = left_vectors.shape[3]
    count_left = left_vectors.shape[1]
    group_width = layout[1]
    site_count = row_count * row_width
    present = vacancy.astype(jnp.float32)
    current = slab_field.reshape(2, group_width, row_count, row_width) * present
    parity_sign = sign_table(row_count, row_width)
    latest = velocity(with_rims(current), parity_sign) * present
    previous = latest
    moment_list = [latest]
    for degree in range(1, MOM):
        applied = haldane(with_rims(latest), parity_sign) * present / BAND_SCALE
        following = applied if degree == 1 else 2.0 * applied - previous
        previous, latest = (latest, following)
        moment_list.append(latest)
    left_matrix = left_vectors.reshape(2 * count_left, site_count)
    summed_list = []
    for moment in moment_list:
        rounded = moment.astype(jnp.bfloat16).reshape(2 * group_width, site_count)
        product = lax.dot_general(
            left_matrix, rounded, (((1,), (1,)), ((), ())), preferred_element_type=jnp.float32
        ).reshape(2, count_left, 2, group_width)
        combined = jnp.stack(
            [product[0, :, 0] + product[1, :, 1], product[0, :, 1] - product[1, :, 0]]
        )
        summed_list.append(lax.psum(combined, "sites"))
    summed = jnp.stack(summed_list, axis=1)
    return summed[..., None]


MESH = pl.DeviceIdType.MESH
HALO = MOM
COLS_AT_ONCE = 16
LANES = 128


def fused_kernel(
    groups, sites, right_ref, left_ref, vacancy_ref, out_ref,
    arrived, field0, field1, field2, field3, present, scaled, doubled, rounded,
    left_held, left_wide, left_flat, partial, shares, total,
    piece_send, piece_recv, rim_send, rim_recv, mask_send, mask_recv,
    share_send, share_recv, total_send, total_recv, left_sem,
):
    chunks, padded_rows, _, wide, width = arrived.shape
    rows = padded_rows - 2 * HALO
    piece = right_ref.shape[5]
    per_row = width // piece
    count = groups * sites
    my_group, my_site = lax.axis_index("cols"), lax.axis_index("sites")
    mine = my_group * sites + my_site
    above, below = lax.rem(my_site + 1, sites), lax.rem(my_site + sites - 1, sites)

    left_copy = pltpu.make_async_copy(left_ref, left_held, left_sem)
    left_copy.start()
    barrier = pltpu.get_barrier_semaphore()

    def greet(step, carry):
        other = lax.rem(mine + step, count)
        pl.semaphore_signal(
            barrier, inc=1, device_id={"cols": other // sites, "sites": lax.rem(other, sites)}, device_id_type=MESH
        )
        return carry

    lax.fori_loop(1, count, greet, 0)

    for row in range(rows):
        present[HALO + row] = jnp.broadcast_to(vacancy_ref[row : row + 1, :].astype(jnp.float32), (8, width))

    pl.semaphore_wait(barrier, count - 1)

    def landing(chunk, run):
        return arrived.at[
            chunk, HALO + run // per_row, :, :, pl.ds(pl.multiple_of(lax.rem(run, per_row) * piece, piece), piece)
        ]

    def piece_of(chunk, group, site):
        return right_ref.at[:, pl.ds(pl.multiple_of(chunk * wide, wide), wide), group, site, 0, :]

    def piece_copy(chunk, step):
        turn = lax.rem(step, 2) * (sites // 2) + step // (2 * groups)
        group = lax.rem(my_group + lax.rem(step // 2, groups), groups)
        site = lax.rem(my_site + turn, sites)
        return pltpu.make_async_remote_copy(
            src_ref=piece_of(chunk, group, site),
            dst_ref=landing(chunk, mine),
            send_sem=piece_send.at[chunk, step],
            recv_sem=piece_recv.at[chunk],
            device_id={"cols": group, "sites": site},
            device_id_type=MESH,
        )

    def rim_copy(source, send_sem, recv_sem, up):
        first = rows if up else HALO
        landing_row = 0 if up else rows + HALO
        return pltpu.make_async_remote_copy(
            src_ref=source.at[pl.ds(first, HALO)],
            dst_ref=source.at[pl.ds(landing_row, HALO)],
            send_sem=send_sem,
            recv_sem=recv_sem,
            device_id={"sites": above if up else below},
            device_id_type=MESH,
        )

    def mask_copies():
        return [rim_copy(present, mask_send.at[i], mask_recv.at[i], up) for i, up in enumerate((True, False))]

    def rim_copies(chunk):
        return [
            rim_copy(arrived.at[chunk], rim_send.at[chunk, i], rim_recv.at[chunk, i], up)
            for i, up in enumerate((True, False))
        ]

    for copy in mask_copies():
        copy.start()

    def send_chunk(chunk, carry):
        def send(step, inner):
            piece_copy(chunk, step).start()
            return inner

        lax.fori_loop(1, count, send, 0)
        pltpu.make_async_copy(piece_of(chunk, my_group, my_site), landing(chunk, mine), piece_recv.at[chunk]).start()
        return carry

    lax.fori_loop(0, min(2, chunks), send_chunk, 0)

    for copy in mask_copies():
        copy.wait()

    def scale_masks(row, carry):
        held = present[row]
        scaled[row] = held * (1.0 / BAND_SCALE)
        doubled[row] = held * (2.0 / BAND_SCALE)
        return carry

    lax.fori_loop(0, padded_rows, scale_masks, 0)

    tiles = [slice(at, at + LANES) for at in range(0, width, LANES)]
    lane = lax.broadcasted_iota(jnp.int32, (8, LANES), 1)
    odd_lane = lax.rem(lane, 2) == 1
    even_sign = jnp.where(odd_lane, -1.0, 1.0)
    nothing = jnp.zeros((8, LANES), jnp.float32)

    def shift(values, offset):
        if offset > 0:
            turned = [pltpu.roll(v, LANES - 1, axis=1) for v in values]
            return [jnp.where(lane == LANES - 1, b, a) for a, b in zip(turned, turned[1:] + [nothing])]
        turned = [pltpu.roll(v, 1, axis=1) for v in values]
        return [jnp.where(lane == 0, b, a) for a, b in zip(turned, [nothing] + turned[:-1])]

    def sweep(source, target, earlier, mask, degree):
        first = degree + 1

        def one_row(row, odd_row):
            sign = -even_sign if odd_row else even_sign
            second, onsite = SECOND_HOP * sign, ONSITE_MASS * sign
            down = odd_lane != odd_row
            factor = [mask[row, :, at] for at in tiles]
            halves = [[], []]
            for part in range(0, wide, 8):
                eight = slice(part, part + 8)
                far, rest = [], []
                for r in (0, 1):
                    centre = [source[row, r, eight, at] for at in tiles]
                    upper = [source[row + 1, r, eight, at] for at in tiles]
                    lower = [source[row - 1, r, eight, at] for at in tiles]
                    right, left = shift(centre, 1), shift(centre, -1)
                    both = [u + l for u, l in zip(upper, lower)]
                    if degree == 0:
                        ahead = shift([2.0 * v - w for v, w in zip(right, both)], 1)
                        behind = shift([2.0 * v - w for v, w in zip(left, both)], -1)
                        far.append([second * (v + w) for v, w in zip(ahead, behind)])
                        rest.append([v - w for v, w in zip(right, left)])
                    else:
                        ahead = shift([v - w for v, w in zip(right, both)], 1)
                        behind = shift([v - w for v, w in zip(left, both)], -1)
                        far.append([second * (v - w) for v, w in zip(ahead, behind)])
                        rest.append([
                            (onsite * c + jnp.where(down, l, u)) + (v + w)
                            for c, u, l, v, w in zip(centre, upper, lower, right, left)
                        ])
                if degree == 0:
                    applied = [
                        [-v - w for v, w in zip(rest[1], far[0])],
                        [v - w for v, w in zip(rest[0], far[1])],
                    ]
                else:
                    applied = [
                        [v - w for v, w in zip(rest[0], far[1])],
                        [v + w for v, w in zip(rest[1], far[0])],
                    ]
                for r in (0, 1):
                    results = [v * f for v, f in zip(applied[r], factor)]
                    if earlier is not None:
                        results = [v - earlier[row, r, eight, at] for v, at in zip(results, tiles)]
                    if target is not None:
                        for v, at in zip(results, tiles):
                            target[row, r, eight, at] = v
                    halves[r].append(results)
            for r in (0, 1):
                base = (r * MOM + degree) * wide
                for i, at in enumerate(tiles):
                    lanes = pl.ds(pl.multiple_of(row * width + at.start, LANES), LANES)
                    block = jnp.concatenate([half[i] for half in halves[r]], axis=0)
                    rounded[base : base + wide, lanes] = block.astype(jnp.bfloat16)

        def pair(step, carry):
            one_row(first + 2 * step, first % 2 == 1)
            one_row(first + 2 * step + 1, first % 2 == 0)
            return carry

        lax.fori_loop(0, (padded_rows - 2 * first) // 2, pair, 0)

    left_copy.wait()

    def widen(step, carry):
        at = pl.ds(pl.multiple_of(step * 16, 16), 16)
        block = left_held[at, :].astype(jnp.float32)
        for i, lanes in enumerate(tiles):
            left_wide[i, at, :] = block[:, lanes]
        return carry

    lax.fori_loop(0, left_ref.shape[0] // 16, widen, 0)
    left_count = left_ref.shape[0] // rows
    for row in range(rows):
        for i, lanes in enumerate(tiles):
            block = left_wide[i, pl.ds(row, left_count, stride=rows), :]
            left_flat[:, row * width + lanes.start : row * width + lanes.stop] = block.astype(jnp.bfloat16)

    def stage(chunk):
        held = arrived.at[chunk, pl.ds(HALO, rows)]
        pltpu.make_async_copy(held, held, piece_recv.at[chunk]).wait()
        for copy in rim_copies(chunk):
            copy.start()

        @pl.when(chunk + 2 < chunks)
        def _():
            send_chunk(chunk + 2, 0)

    def compute(chunk):
        for copy in rim_copies(chunk):
            copy.wait()

        def mask_row(row, carry):
            for r in (0, 1):
                for part in range(0, wide, 8):
                    at = slice(part, part + 8)
                    field0[row, r, at, :] = arrived[chunk, row, r, at, :] * present[row]
            return carry

        lax.fori_loop(0, padded_rows, mask_row, 0)
        sweep(field0, field1, None, present, 0)
        sweep(field1, field2, None, scaled, 1)
        sweep(field2, field3, field1, doubled, 2)
        sweep(field3, None, field2, doubled, 3)
        product = lax.dot_general(
            left_flat[...],
            rounded[:, HALO * width : (HALO + rows) * width],
            (((1,), (1,)), ((), ())),
            preferred_element_type=jnp.float32,
        )
        count_left = product.shape[0] // 2
        half = product.shape[1] // 2
        real, imaginary = product[:count_left], product[count_left:]
        swapped = pltpu.roll(imaginary, half, axis=1)
        wheres = lax.broadcasted_iota(jnp.int32, swapped.shape, 1)
        combined = real + jnp.where(wheres < half, swapped, -swapped)
        partial[pl.ds(pl.multiple_of(chunk * count_left, count_left), count_left), :] = combined

    def step_chunk(step, carry):
        @pl.when(step < chunks)
        def _():
            stage(step)

        @pl.when(step > 0)
        def _():
            compute(step - 1)

        return carry

    lax.fori_loop(0, chunks + 1, step_chunk, 0)

    share_rows = shares.shape[1]

    def rows_of(site):
        return pl.ds(pl.multiple_of(site * share_rows, share_rows), share_rows)

    def share_copy(step):
        site = lax.rem(my_site + step, sites)
        return pltpu.make_async_remote_copy(
            src_ref=partial.at[rows_of(site)],
            dst_ref=shares.at[my_site],
            send_sem=share_send.at[step],
            recv_sem=share_recv,
            device_id={"sites": site},
            device_id_type=MESH,
        )

    def total_copy(step):
        site = lax.rem(my_site + step, sites)
        return pltpu.make_async_remote_copy(
            src_ref=total.at[rows_of(my_site)],
            dst_ref=total.at[rows_of(my_site)],
            send_sem=total_send.at[step],
            recv_sem=total_recv,
            device_id={"sites": site},
            device_id_type=MESH,
        )

    def start_all(make, stop):
        def go(step, carry):
            make(step).start()
            return carry

        lax.fori_loop(1, stop, go, 0)

    def sent_all(make, stop):
        def go(step, carry):
            make(step).wait_send()
            return carry

        lax.fori_loop(1, stop, go, 0)

    start_all(share_copy, sites)
    pltpu.make_async_copy(partial.at[rows_of(my_site)], shares.at[my_site], share_recv).start()
    pltpu.make_async_copy(shares, shares, share_recv).wait()
    summed = shares[0]
    for site in range(1, sites):
        summed = summed + shares[site]
    total[rows_of(my_site), :] = summed
    start_all(total_copy, sites)
    whole = total.at[pl.ds(0, (sites - 1) * share_rows)]
    pltpu.make_async_copy(whole, whole, total_recv).wait()
    out_ref[...] = total[...]
    sent_all(share_copy, sites)
    sent_all(total_copy, sites)

    def sent_chunk(chunk, carry):
        sent_all(functools.partial(piece_copy, chunk), count)
        return carry

    lax.fori_loop(0, chunks, sent_chunk, 0)


def per_device_fused(groups, sites, right_vectors, left_vectors, vacancy):
    width_group = right_vectors.shape[1]
    count_left, rows, width = left_vectors.shape[1:]
    wide = COLS_AT_ONCE
    chunks = width_group // wide
    padded = rows + 2 * HALO
    field = pltpu.VMEM((padded, 2, wide, width), jnp.float32)
    mask = pltpu.VMEM((padded, 8, width), jnp.float32)
    sums = (chunks * count_left, 2 * MOM * wide)
    dma = pltpu.SemaphoreType.DMA
    call = pl.pallas_call(
        functools.partial(fused_kernel, groups, sites),
        out_shape=jax.ShapeDtypeStruct(sums, jnp.float32),
        in_specs=[
            pl.BlockSpec(memory_space=pl.ANY),
            pl.BlockSpec(memory_space=pl.ANY),
            pl.BlockSpec(memory_space=pltpu.VMEM),
        ],
        out_specs=pl.BlockSpec(memory_space=pltpu.VMEM),
        scratch_shapes=[
            pltpu.VMEM((chunks, padded, 2, wide, width), jnp.float32),
            field, field, field, field, mask, mask, mask,
            pltpu.VMEM((2 * MOM * wide, padded * width), jnp.bfloat16),
            pltpu.VMEM((2 * count_left * rows, width), jnp.bfloat16),
            pltpu.VMEM((width // LANES, 2 * count_left * rows, LANES), jnp.float32),
            pltpu.VMEM((2 * count_left, rows * width), jnp.bfloat16),
            pltpu.VMEM(sums, jnp.float32),
            pltpu.VMEM((sites, sums[0] // sites, sums[1]), jnp.float32),
            pltpu.VMEM(sums, jnp.float32),
            dma((chunks, groups * sites)), dma((chunks,)),
            dma((chunks, 2)), dma((chunks, 2)), dma((2,)), dma((2,)),
            dma((sites,)), dma, dma((sites,)), dma, dma,
        ],
        compiler_params=pltpu.CompilerParams(
            collective_id=0, has_side_effects=True, vmem_limit_bytes=48 * 1024 * 1024
        ),
        cost_estimate=pl.CostEstimate(flops=2 * 10**9, bytes_accessed=8 * 10**6, transcendentals=0),
    )
    summed = call(right_vectors, left_vectors.reshape(2 * count_left * rows, width), vacancy)
    summed = summed.reshape(chunks, count_left, 2, MOM, wide)
    return summed.transpose(2, 3, 1, 0, 4).reshape(2, MOM, count_left, width_group, 1)


def per_device(groups, sites, right_vectors, left_vectors, vacancy):
    columns, piece = right_vectors.shape[1], right_vectors.shape[5]
    count_left, rows, width = left_vectors.shape[1:]
    shares = (columns // COLS_AT_ONCE) * count_left
    fits = (
        piece % 128 == 0 and width % piece == 0 and right_vectors.shape[4] == 1
        and columns % COLS_AT_ONCE == 0 and rows % 2 == 0 and rows >= HALO
        and sites >= 4 and sites % 2 == 0 and shares % (8 * sites) == 0 and count_left % 8 == 0 and (2 * count_left * rows) % 16 == 0
    )
    if fits:
        return per_device_fused(groups, sites, right_vectors, left_vectors, vacancy)
    return per_device_plain(right_vectors, left_vectors, vacancy)


def solution(mesh):
    return jax.shard_map(
        functools.partial(per_device, mesh.shape["cols"], mesh.shape["sites"]),
        mesh=mesh,
        in_specs=(
            P(None, None, None, None, ("cols", "sites"), None),
            P(None, None, "sites", None),
            P("sites", None),
        ),
        out_specs=P(None, None, None, None, "cols"),
        check_vma=False,
    )
```

```python
import functools

import jax
import jax.numpy as jnp
from jax import lax
from jax.experimental import pallas as pl
from jax.experimental.pallas import tpu as pltpu
from jax.sharding import PartitionSpec as P

MOM = 4


ONSITE_MASS = 0.3
SECOND_HOP = 0.2
BAND_SCALE = 4.5


def padded_2(cells, sides, width):
    for axis, dim in sides:
        count = lax.axis_size(axis)
        head = lax.slice_in_dim(cells, 0, width, axis=dim)
        tail = lax.slice_in_dim(cells, cells.shape[dim] - width, cells.shape[dim], axis=dim)
        cells = jnp.concatenate(
            [
                lax.ppermute(tail, axis, [(i, (i + 1) % count) for i in range(count)]),
                cells,
                lax.ppermute(head, axis, [((i + 1) % count, i) for i in range(count)]),
            ],
            axis=dim,
        )
    return cells


def column_shift(values, offset):
    row_width = values.shape[-1]
    filler = jnp.zeros(values.shape[:-1] + (abs(offset),), values.dtype)
    if offset > 0:
        return jnp.concatenate([values[..., offset:], filler], axis=-1)
    return jnp.concatenate([filler, values[..., : row_width + offset]], axis=-1)


def rotate_phase(values):
    return jnp.stack([-values[1], values[0]])


def sign_table(row_count, row_width):
    rows_index = lax.broadcasted_iota(jnp.int32, (row_count, row_width), 0)
    cols_index = lax.broadcasted_iota(jnp.int32, (row_count, row_width), 1)
    return (1 - 2 * ((rows_index + cols_index) % 2)).astype(jnp.float32)


def haldane(padded, parity_sign):
    centre = padded[:, :, 1:-1, :]
    upper_row = padded[:, :, 2:, :]
    lower_row = padded[:, :, :-2, :]
    vertical = jnp.where(parity_sign > 0, upper_row, lower_row)
    nearest = column_shift(centre, 1) + column_shift(centre, -1) + vertical
    second = (
        column_shift(centre, 2)
        - column_shift(centre, -2)
        + column_shift(upper_row, -1)
        - column_shift(lower_row, 1)
        + column_shift(lower_row, -1)
        - column_shift(upper_row, 1)
    )
    return (
        ONSITE_MASS * parity_sign * centre
        + nearest
        + SECOND_HOP * parity_sign * rotate_phase(second)
    )


def velocity(padded, parity_sign):
    centre = padded[:, :, 1:-1, :]
    upper_row = padded[:, :, 2:, :]
    lower_row = padded[:, :, :-2, :]
    along_x = column_shift(centre, 1) - column_shift(centre, -1)
    farther = column_shift(centre, 2) + column_shift(centre, -2)
    diagonal = (
        column_shift(upper_row, 1)
        + column_shift(upper_row, -1)
        + column_shift(lower_row, 1)
        + column_shift(lower_row, -1)
    )
    return rotate_phase(along_x) - SECOND_HOP * parity_sign * (2.0 * farther - diagonal)


def with_rims(values):
    return padded_2(values, (("sites", 2),), 1)


def per_device_plain(right_vectors, left_vectors, vacancy):
    layout = right_vectors.shape
    pieces = right_vectors.reshape(layout[0], layout[1], layout[2], layout[3], layout[5])
    slab_field = lax.all_to_all(
        lax.all_to_all(pieces, "cols", split_axis=2, concat_axis=2, tiled=True),
        "sites",
        split_axis=3,
        concat_axis=3,
        tiled=True,
    )
    row_count = left_vectors.shape[2]
    row_width = left_vectors.shape[3]
    count_left = left_vectors.shape[1]
    group_width = layout[1]
    site_count = row_count * row_width
    present = vacancy.astype(jnp.float32)
    current = slab_field.reshape(2, group_width, row_count, row_width) * present
    parity_sign = sign_table(row_count, row_width)
    latest = velocity(with_rims(current), parity_sign) * present
    previous = latest
    moment_list = [latest]
    for degree in range(1, MOM):
        applied = haldane(with_rims(latest), parity_sign) * present / BAND_SCALE
        following = applied if degree == 1 else 2.0 * applied - previous
        previous, latest = (latest, following)
        moment_list.append(latest)
    left_matrix = left_vectors.reshape(2 * count_left, site_count)
    summed_list = []
    for moment in moment_list:
        rounded = moment.astype(jnp.bfloat16).reshape(2 * group_width, site_count)
        product = lax.dot_general(
            left_matrix, rounded, (((1,), (1,)), ((), ())), preferred_element_type=jnp.float32
        ).reshape(2, count_left, 2, group_width)
        combined = jnp.stack(
            [product[0, :, 0] + product[1, :, 1], product[0, :, 1] - product[1, :, 0]]
        )
        summed_list.append(lax.psum(combined, "sites"))
    summed = jnp.stack(summed_list, axis=1)
    return summed[..., None]


MESH = pl.DeviceIdType.MESH
HALO = MOM
COLS_AT_ONCE = 16
LANES = 128


def fused_kernel(
    groups, sites, right_ref, left_ref, vacancy_ref, out_ref,
    arrived, field0, field1, field2, field3, present, scaled, doubled, rounded,
    staged, left_held, left_wide, left_flat, partial, shares, total,
    piece_send, piece_recv, rim_send, rim_recv, mask_send, mask_recv,
    share_send, share_recv, total_send, total_recv, left_sem, stage_sem,
):
    chunks, padded_rows, per_row, _, wide, piece = arrived.shape
    width = per_row * piece
    rows = padded_rows - 2 * HALO
    count = groups * sites
    my_group, my_site = lax.axis_index("cols"), lax.axis_index("sites")
    mine = my_group * sites + my_site
    above, below = lax.rem(my_site + 1, sites), lax.rem(my_site + sites - 1, sites)

    def piece_of(chunk, group, site):
        return right_ref.at[:, pl.ds(pl.multiple_of(chunk * wide, wide), wide), group, site, 0, :]

    def lay_out(chunk, carry):
        def place(other, inner):
            pltpu.make_async_copy(
                piece_of(chunk, other // sites, lax.rem(other, sites)), staged.at[chunk, other], stage_sem.at[chunk]
            ).start()
            return inner

        lax.fori_loop(0, count, place, 0)
        return carry

    left_copy = pltpu.make_async_copy(left_ref, left_held, left_sem)
    left_copy.start()
    barrier = pltpu.get_barrier_semaphore()

    def greet(step, carry):
        other = lax.rem(mine + step, count)
        pl.semaphore_signal(
            barrier, inc=1, device_id={"cols": other // sites, "sites": lax.rem(other, sites)}, device_id_type=MESH
        )
        return carry

    lax.fori_loop(1, count, greet, 0)
    lay_out(0, 0)

    for row in range(rows):
        present[HALO + row] = jnp.broadcast_to(vacancy_ref[row : row + 1, :].astype(jnp.float32), (8, width))

    pl.semaphore_wait(barrier, count - 1)

    def landing(chunk, run):
        return arrived.at[chunk, HALO + run // per_row, lax.rem(run, per_row)]

    def piece_copy(chunk, step):
        turn = lax.rem(step, 2) * (sites // 2) + step // (2 * groups)
        group = lax.rem(my_group + lax.rem(step // 2, groups), groups)
        site = lax.rem(my_site + turn, sites)
        return pltpu.make_async_remote_copy(
            src_ref=staged.at[chunk, group * sites + site],
            dst_ref=landing(chunk, mine),
            send_sem=piece_send.at[chunk, step],
            recv_sem=piece_recv.at[chunk],
            device_id={"cols": group, "sites": site},
            device_id_type=MESH,
        )

    def rim_copy(source, send_sem, recv_sem, up):
        first = rows if up else HALO
        landing_row = 0 if up else rows + HALO
        return pltpu.make_async_remote_copy(
            src_ref=source.at[pl.ds(first, HALO)],
            dst_ref=source.at[pl.ds(landing_row, HALO)],
            send_sem=send_sem,
            recv_sem=recv_sem,
            device_id={"sites": above if up else below},
            device_id_type=MESH,
        )

    def mask_copies():
        return [rim_copy(present, mask_send.at[i], mask_recv.at[i], up) for i, up in enumerate((True, False))]

    def rim_copies(chunk):
        return [
            rim_copy(arrived.at[chunk], rim_send.at[chunk, i], rim_recv.at[chunk, i], up)
            for i, up in enumerate((True, False))
        ]

    for copy in mask_copies():
        copy.start()

    def send_chunk(chunk, carry):
        pltpu.make_async_copy(staged.at[chunk], staged.at[chunk], stage_sem.at[chunk]).wait()

        def send(step, inner):
            piece_copy(chunk, step).start()
            return inner

        lax.fori_loop(1, count, send, 0)
        pltpu.make_async_copy(staged.at[chunk, mine], landing(chunk, mine), piece_recv.at[chunk]).start()
        return carry

    send_chunk(0, 0)
    lax.fori_loop(1, chunks, lay_out, 0)
    lax.fori_loop(1, min(2, chunks), send_chunk, 0)

    for copy in mask_copies():
        copy.wait()

    def scale_masks(row, carry):
        held = present[row]
        scaled[row] = held * (1.0 / BAND_SCALE)
        doubled[row] = held * (2.0 / BAND_SCALE)
        return carry

    lax.fori_loop(0, padded_rows, scale_masks, 0)

    tiles = [slice(at, at + LANES) for at in range(0, width, LANES)]
    lane = lax.broadcasted_iota(jnp.int32, (8, LANES), 1)
    odd_lane = lax.rem(lane, 2) == 1
    even_sign = jnp.where(odd_lane, -1.0, 1.0)
    nothing = jnp.zeros((8, LANES), jnp.float32)

    def shift(values, offset):
        if offset > 0:
            turned = [pltpu.roll(v, LANES - 1, axis=1) for v in values]
            return [jnp.where(lane == LANES - 1, b, a) for a, b in zip(turned, turned[1:] + [nothing])]
        turned = [pltpu.roll(v, 1, axis=1) for v in values]
        return [jnp.where(lane == 0, b, a) for a, b in zip(turned, [nothing] + turned[:-1])]

    def sweep(source, target, earlier, mask, degree):
        first = degree + 1

        def one_row(row, odd_row):
            sign = -even_sign if odd_row else even_sign
            second, onsite = SECOND_HOP * sign, ONSITE_MASS * sign
            down = odd_lane != odd_row
            factor = [mask[row, :, at] for at in tiles]
            halves = [[], []]
            for part in range(0, wide, 8):
                eight = slice(part, part + 8)
                far, rest = [], []
                for r in (0, 1):
                    centre = [source[row, r, eight, at] for at in tiles]
                    upper = [source[row + 1, r, eight, at] for at in tiles]
                    lower = [source[row - 1, r, eight, at] for at in tiles]
                    right, left = shift(centre, 1), shift(centre, -1)
                    both = [u + l for u, l in zip(upper, lower)]
                    if degree == 0:
                        ahead = shift([2.0 * v - w for v, w in zip(right, both)], 1)
                        behind = shift([2.0 * v - w for v, w in zip(left, both)], -1)
                        far.append([second * (v + w) for v, w in zip(ahead, behind)])
                        rest.append([v - w for v, w in zip(right, left)])
                    else:
                        ahead = shift([v - w for v, w in zip(right, both)], 1)
                        behind = shift([v - w for v, w in zip(left, both)], -1)
                        far.append([second * (v - w) for v, w in zip(ahead, behind)])
                        rest.append([
                            (onsite * c + jnp.where(down, l, u)) + (v + w)
                            for c, u, l, v, w in zip(centre, upper, lower, right, left)
                        ])
                if degree == 0:
                    applied = [
                        [-v - w for v, w in zip(rest[1], far[0])],
                        [v - w for v, w in zip(rest[0], far[1])],
                    ]
                else:
                    applied = [
                        [v - w for v, w in zip(rest[0], far[1])],
                        [v + w for v, w in zip(rest[1], far[0])],
                    ]
                for r in (0, 1):
                    results = [v * f for v, f in zip(applied[r], factor)]
                    if earlier is not None:
                        results = [v - earlier[row, r, eight, at] for v, at in zip(results, tiles)]
                    if target is not None:
                        for v, at in zip(results, tiles):
                            target[row, r, eight, at] = v
                    halves[r].append(results)
            for r in (0, 1):
                base = (r * MOM + degree) * wide
                for i, at in enumerate(tiles):
                    lanes = pl.ds(pl.multiple_of(row * width + at.start, LANES), LANES)
                    block = jnp.concatenate([half[i] for half in halves[r]], axis=0)
                    rounded[base : base + wide, lanes] = block.astype(jnp.bfloat16)

        def pair(step, carry):
            one_row(first + 2 * step, first % 2 == 1)
            one_row(first + 2 * step + 1, first % 2 == 0)
            return carry

        lax.fori_loop(0, (padded_rows - 2 * first) // 2, pair, 0)

    left_copy.wait()

    def widen(step, carry):
        at = pl.ds(pl.multiple_of(step * 16, 16), 16)
        block = left_held[at, :].astype(jnp.float32)
        for i, lanes in enumerate(tiles):
            left_wide[i, at, :] = block[:, lanes]
        return carry

    lax.fori_loop(0, left_ref.shape[0] // 16, widen, 0)
    left_count = left_ref.shape[0] // rows
    for row in range(rows):
        for i, lanes in enumerate(tiles):
            block = left_wide[i, pl.ds(row, left_count, stride=rows), :]
            left_flat[:, row * width + lanes.start : row * width + lanes.stop] = block.astype(jnp.bfloat16)

    def stage(chunk):
        held = arrived.at[chunk, pl.ds(HALO, rows)]
        pltpu.make_async_copy(held, held, piece_recv.at[chunk]).wait()
        for copy in rim_copies(chunk):
            copy.start()

        @pl.when(chunk + 2 < chunks)
        def _():
            send_chunk(chunk + 2, 0)

    def compute(chunk):
        for copy in rim_copies(chunk):
            copy.wait()

        def mask_row(row, carry):
            for r in (0, 1):
                for part in range(0, wide, 8):
                    at = slice(part, part + 8)
                    for run in range(per_row):
                        lanes = slice(run * piece, (run + 1) * piece)
                        field0[row, r, at, lanes] = arrived[chunk, row, run, r, at, :] * present[row, :, lanes]
            return carry

        lax.fori_loop(0, padded_rows, mask_row, 0)
        sweep(field0, field1, None, present, 0)
        sweep(field1, field2, None, scaled, 1)
        sweep(field2, field3, field1, doubled, 2)
        sweep(field3, None, field2, doubled, 3)
        product = lax.dot_general(
            left_flat[...],
            rounded[:, HALO * width : (HALO + rows) * width],
            (((1,), (1,)), ((), ())),
            preferred_element_type=jnp.float32,
        )
        count_left = product.shape[0] // 2
        half = product.shape[1] // 2
        real, imaginary = product[:count_left], product[count_left:]
        swapped = pltpu.roll(imaginary, half, axis=1)
        wheres = lax.broadcasted_iota(jnp.int32, swapped.shape, 1)
        combined = real + jnp.where(wheres < half, swapped, -swapped)
        partial[pl.ds(pl.multiple_of(chunk * count_left, count_left), count_left), :] = combined

    def step_chunk(step, carry):
        @pl.when(step < chunks)
        def _():
            stage(step)

        @pl.when(step > 0)
        def _():
            compute(step - 1)

        return carry

    lax.fori_loop(0, chunks + 1, step_chunk, 0)

    share_rows = shares.shape[1]

    def rows_of(site):
        return pl.ds(pl.multiple_of(site * share_rows, share_rows), share_rows)

    def share_copy(step):
        site = lax.rem(my_site + step, sites)
        return pltpu.make_async_remote_copy(
            src_ref=partial.at[rows_of(site)],
            dst_ref=shares.at[my_site],
            send_sem=share_send.at[step],
            recv_sem=share_recv,
            device_id={"sites": site},
            device_id_type=MESH,
        )

    def total_copy(step):
        site = lax.rem(my_site + step, sites)
        return pltpu.make_async_remote_copy(
            src_ref=total.at[rows_of(my_site)],
            dst_ref=total.at[rows_of(my_site)],
            send_sem=total_send.at[step],
            recv_sem=total_recv,
            device_id={"sites": site},
            device_id_type=MESH,
        )

    def start_all(make, stop):
        def go(step, carry):
            make(step).start()
            return carry

        lax.fori_loop(1, stop, go, 0)

    def sent_all(make, stop):
        def go(step, carry):
            make(step).wait_send()
            return carry

        lax.fori_loop(1, stop, go, 0)

    start_all(share_copy, sites)
    pltpu.make_async_copy(partial.at[rows_of(my_site)], shares.at[my_site], share_recv).start()
    pltpu.make_async_copy(shares, shares, share_recv).wait()
    summed = shares[0]
    for site in range(1, sites):
        summed = summed + shares[site]
    total[rows_of(my_site), :] = summed
    start_all(total_copy, sites)
    whole = total.at[pl.ds(0, (sites - 1) * share_rows)]
    pltpu.make_async_copy(whole, whole, total_recv).wait()
    out_ref[...] = total[...]
    sent_all(share_copy, sites)
    sent_all(total_copy, sites)

    def sent_chunk(chunk, carry):
        sent_all(functools.partial(piece_copy, chunk), count)
        return carry

    lax.fori_loop(0, chunks, sent_chunk, 0)


def per_device_fused(groups, sites, right_vectors, left_vectors, vacancy):
    width_group, piece = right_vectors.shape[1], right_vectors.shape[5]
    count_left, rows, width = left_vectors.shape[1:]
    wide = COLS_AT_ONCE
    chunks = width_group // wide
    padded = rows + 2 * HALO
    field = pltpu.VMEM((padded, 2, wide, width), jnp.float32)
    mask = pltpu.VMEM((padded, 8, width), jnp.float32)
    sums = (chunks * count_left, 2 * MOM * wide)
    dma = pltpu.SemaphoreType.DMA
    call = pl.pallas_call(
        functools.partial(fused_kernel, groups, sites),
        out_shape=jax.ShapeDtypeStruct(sums, jnp.float32),
        in_specs=[
            pl.BlockSpec(memory_space=pltpu.HBM),
            pl.BlockSpec(memory_space=pltpu.HBM),
            pl.BlockSpec(memory_space=pltpu.VMEM),
        ],
        out_specs=pl.BlockSpec(memory_space=pltpu.VMEM),
        scratch_shapes=[
            pltpu.VMEM((chunks, padded, width // piece, 2, wide, piece), jnp.float32),
            field, field, field, field, mask, mask, mask,
            pltpu.VMEM((2 * MOM * wide, padded * width), jnp.bfloat16),
            pltpu.VMEM((chunks, groups * sites, 2, wide, piece), jnp.float32),
            pltpu.VMEM((2 * count_left * rows, width), jnp.bfloat16),
            pltpu.VMEM((width // LANES, 2 * count_left * rows, LANES), jnp.float32),
            pltpu.VMEM((2 * count_left, rows * width), jnp.bfloat16),
            pltpu.VMEM(sums, jnp.float32),
            pltpu.VMEM((sites, sums[0] // sites, sums[1]), jnp.float32),
            pltpu.VMEM(sums, jnp.float32),
            dma((chunks, groups * sites)), dma((chunks,)),
            dma((chunks, 2)), dma((chunks, 2)), dma((2,)), dma((2,)),
            dma((sites,)), dma, dma((sites,)), dma, dma, dma((chunks,)),
        ],
        compiler_params=pltpu.CompilerParams(
            collective_id=0, has_side_effects=True, vmem_limit_bytes=125 * 512 * 1024
        ),
        cost_estimate=pl.CostEstimate(flops=2 * 10**9, bytes_accessed=8 * 10**6, transcendentals=0),
    )
    summed = call(right_vectors, left_vectors.reshape(2 * count_left * rows, width), vacancy)
    summed = summed.reshape(chunks, count_left, 2, MOM, wide)
    return summed.transpose(2, 3, 1, 0, 4).reshape(2, MOM, count_left, width_group, 1)


def per_device(groups, sites, right_vectors, left_vectors, vacancy):
    columns, piece = right_vectors.shape[1], right_vectors.shape[5]
    count_left, rows, width = left_vectors.shape[1:]
    shares = (columns // COLS_AT_ONCE) * count_left
    fits = (
        piece % 128 == 0 and width % piece == 0 and right_vectors.shape[4] == 1
        and columns % COLS_AT_ONCE == 0 and rows % 2 == 0 and rows >= HALO
        and sites >= 4 and sites % 2 == 0 and shares % (8 * sites) == 0 and count_left % 8 == 0 and (2 * count_left * rows) % 16 == 0
    )
    if fits:
        return per_device_fused(groups, sites, right_vectors, left_vectors, vacancy)
    return per_device_plain(right_vectors, left_vectors, vacancy)


def solution(mesh):
    return jax.shard_map(
        functools.partial(per_device, mesh.shape["cols"], mesh.shape["sites"]),
        mesh=mesh,
        in_specs=(
            P(None, None, None, None, ("cols", "sites"), None),
            P(None, None, "sites", None),
            P("sites", None),
        ),
        out_specs=P(None, None, None, None, "cols"),
        check_vma=False,
    )
```

```python
import functools

import jax
import jax.numpy as jnp
from jax import lax
from jax.experimental import pallas as pl
from jax.experimental.pallas import tpu as pltpu
from jax.sharding import PartitionSpec as P

MOM = 4


ONSITE_MASS = 0.3
SECOND_HOP = 0.2
BAND_SCALE = 4.5


def padded_2(cells, sides, width):
    for axis, dim in sides:
        count = lax.axis_size(axis)
        head = lax.slice_in_dim(cells, 0, width, axis=dim)
        tail = lax.slice_in_dim(cells, cells.shape[dim] - width, cells.shape[dim], axis=dim)
        cells = jnp.concatenate(
            [
                lax.ppermute(tail, axis, [(i, (i + 1) % count) for i in range(count)]),
                cells,
                lax.ppermute(head, axis, [((i + 1) % count, i) for i in range(count)]),
            ],
            axis=dim,
        )
    return cells


def column_shift(values, offset):
    row_width = values.shape[-1]
    filler = jnp.zeros(values.shape[:-1] + (abs(offset),), values.dtype)
    if offset > 0:
        return jnp.concatenate([values[..., offset:], filler], axis=-1)
    return jnp.concatenate([filler, values[..., : row_width + offset]], axis=-1)


def rotate_phase(values):
    return jnp.stack([-values[1], values[0]])


def sign_table(row_count, row_width):
    rows_index = lax.broadcasted_iota(jnp.int32, (row_count, row_width), 0)
    cols_index = lax.broadcasted_iota(jnp.int32, (row_count, row_width), 1)
    return (1 - 2 * ((rows_index + cols_index) % 2)).astype(jnp.float32)


def haldane(padded, parity_sign):
    centre = padded[:, :, 1:-1, :]
    upper_row = padded[:, :, 2:, :]
    lower_row = padded[:, :, :-2, :]
    vertical = jnp.where(parity_sign > 0, upper_row, lower_row)
    nearest = column_shift(centre, 1) + column_shift(centre, -1) + vertical
    second = (
        column_shift(centre, 2)
        - column_shift(centre, -2)
        + column_shift(upper_row, -1)
        - column_shift(lower_row, 1)
        + column_shift(lower_row, -1)
        - column_shift(upper_row, 1)
    )
    return (
        ONSITE_MASS * parity_sign * centre
        + nearest
        + SECOND_HOP * parity_sign * rotate_phase(second)
    )


def velocity(padded, parity_sign):
    centre = padded[:, :, 1:-1, :]
    upper_row = padded[:, :, 2:, :]
    lower_row = padded[:, :, :-2, :]
    along_x = column_shift(centre, 1) - column_shift(centre, -1)
    farther = column_shift(centre, 2) + column_shift(centre, -2)
    diagonal = (
        column_shift(upper_row, 1)
        + column_shift(upper_row, -1)
        + column_shift(lower_row, 1)
        + column_shift(lower_row, -1)
    )
    return rotate_phase(along_x) - SECOND_HOP * parity_sign * (2.0 * farther - diagonal)


def with_rims(values):
    return padded_2(values, (("sites", 2),), 1)


def per_device_plain(right_vectors, left_vectors, vacancy):
    layout = right_vectors.shape
    pieces = right_vectors.reshape(layout[0], layout[1], layout[2], layout[3], layout[5])
    slab_field = lax.all_to_all(
        lax.all_to_all(pieces, "cols", split_axis=2, concat_axis=2, tiled=True),
        "sites",
        split_axis=3,
        concat_axis=3,
        tiled=True,
    )
    row_count = left_vectors.shape[2]
    row_width = left_vectors.shape[3]
    count_left = left_vectors.shape[1]
    group_width = layout[1]
    site_count = row_count * row_width
    present = vacancy.astype(jnp.float32)
    current = slab_field.reshape(2, group_width, row_count, row_width) * present
    parity_sign = sign_table(row_count, row_width)
    latest = velocity(with_rims(current), parity_sign) * present
    previous = latest
    moment_list = [latest]
    for degree in range(1, MOM):
        applied = haldane(with_rims(latest), parity_sign) * present / BAND_SCALE
        following = applied if degree == 1 else 2.0 * applied - previous
        previous, latest = (latest, following)
        moment_list.append(latest)
    left_matrix = left_vectors.reshape(2 * count_left, site_count)
    summed_list = []
    for moment in moment_list:
        rounded = moment.astype(jnp.bfloat16).reshape(2 * group_width, site_count)
        product = lax.dot_general(
            left_matrix, rounded, (((1,), (1,)), ((), ())), preferred_element_type=jnp.float32
        ).reshape(2, count_left, 2, group_width)
        combined = jnp.stack(
            [product[0, :, 0] + product[1, :, 1], product[0, :, 1] - product[1, :, 0]]
        )
        summed_list.append(lax.psum(combined, "sites"))
    summed = jnp.stack(summed_list, axis=1)
    return summed[..., None]


MESH = pl.DeviceIdType.MESH
HALO = MOM
COLS_AT_ONCE = 16
LANES = 128


def fused_kernel(
    groups, sites, right_ref, left_ref, vacancy_ref, out_ref,
    arrived, field0, field1, field2, field3, present, scaled, doubled, rounded,
    staged, left_held, left_wide, left_flat, partial, shares, total,
    piece_send, piece_recv, rim_send, rim_recv, mask_send, mask_recv,
    share_send, share_recv, total_send, total_recv, left_sem, stage_sem,
):
    chunks, padded_rows, per_row, _, wide, piece = arrived.shape
    width = per_row * piece
    rows = padded_rows - 2 * HALO
    count = groups * sites
    my_group, my_site = lax.axis_index("cols"), lax.axis_index("sites")
    mine = my_group * sites + my_site
    above, below = lax.rem(my_site + 1, sites), lax.rem(my_site + sites - 1, sites)

    def piece_of(chunk, group, site):
        return right_ref.at[:, pl.ds(pl.multiple_of(chunk * wide, wide), wide), group, site, 0, :]

    def lay_out(chunk, carry):
        def place(other, inner):
            pltpu.make_async_copy(
                piece_of(chunk, other // sites, lax.rem(other, sites)), staged.at[chunk, other], stage_sem.at[chunk]
            ).start()
            return inner

        lax.fori_loop(0, count, place, 0)
        return carry

    left_copy = pltpu.make_async_copy(left_ref, left_held, left_sem)
    left_copy.start()
    barrier = pltpu.get_barrier_semaphore()

    def greet(step, carry):
        other = lax.rem(mine + step, count)
        pl.semaphore_signal(
            barrier, inc=1, device_id={"cols": other // sites, "sites": lax.rem(other, sites)}, device_id_type=MESH
        )
        return carry

    lax.fori_loop(1, count, greet, 0)
    lay_out(0, 0)

    for row in range(rows):
        present[HALO + row] = jnp.broadcast_to(vacancy_ref[row : row + 1, :].astype(jnp.float32), (8, width))

    pl.semaphore_wait(barrier, count - 1)

    def landing(chunk, run):
        return arrived.at[chunk, HALO + run // per_row, lax.rem(run, per_row)]

    def piece_copy(chunk, step):
        turn = lax.rem(step, 2) * (sites // 2) + step // (2 * groups)
        group = lax.rem(my_group + lax.rem(step // 2, groups), groups)
        site = lax.rem(my_site + turn, sites)
        return pltpu.make_async_remote_copy(
            src_ref=staged.at[chunk, group * sites + site],
            dst_ref=landing(chunk, mine),
            send_sem=piece_send.at[chunk, step],
            recv_sem=piece_recv.at[chunk],
            device_id={"cols": group, "sites": site},
            device_id_type=MESH,
        )

    def rim_copy(source, send_sem, recv_sem, up):
        first = rows if up else HALO
        landing_row = 0 if up else rows + HALO
        return pltpu.make_async_remote_copy(
            src_ref=source.at[pl.ds(first, HALO)],
            dst_ref=source.at[pl.ds(landing_row, HALO)],
            send_sem=send_sem,
            recv_sem=recv_sem,
            device_id={"sites": above if up else below},
            device_id_type=MESH,
        )

    def mask_copies():
        return [rim_copy(present, mask_send.at[i], mask_recv.at[i], up) for i, up in enumerate((True, False))]

    def rim_copies(chunk):
        return [
            rim_copy(arrived.at[chunk], rim_send.at[chunk, i], rim_recv.at[chunk, i], up)
            for i, up in enumerate((True, False))
        ]

    for copy in mask_copies():
        copy.start()

    def send_chunk(chunk, carry):
        pltpu.make_async_copy(staged.at[chunk], staged.at[chunk], stage_sem.at[chunk]).wait()

        def send(step, inner):
            @pl.when(chunk > 0)
            def _():
                piece_copy(chunk - 1, step).wait_send()

            piece_copy(chunk, step).start()
            return inner

        lax.fori_loop(1, count, send, 0)
        pltpu.make_async_copy(staged.at[chunk, mine], landing(chunk, mine), piece_recv.at[chunk]).start()
        return carry

    send_chunk(0, 0)
    lax.fori_loop(1, chunks, lay_out, 0)

    for copy in mask_copies():
        copy.wait()

    def scale_masks(row, carry):
        held = present[row]
        scaled[row] = held * (1.0 / BAND_SCALE)
        doubled[row] = held * (2.0 / BAND_SCALE)
        return carry

    lax.fori_loop(0, padded_rows, scale_masks, 0)

    tiles = [slice(at, at + LANES) for at in range(0, width, LANES)]
    lane = lax.broadcasted_iota(jnp.int32, (8, LANES), 1)
    odd_lane = lax.rem(lane, 2) == 1
    even_sign = jnp.where(odd_lane, -1.0, 1.0)
    nothing = jnp.zeros((8, LANES), jnp.float32)

    def shift(values, offset):
        if offset > 0:
            turned = [pltpu.roll(v, LANES - 1, axis=1) for v in values]
            return [jnp.where(lane == LANES - 1, b, a) for a, b in zip(turned, turned[1:] + [nothing])]
        turned = [pltpu.roll(v, 1, axis=1) for v in values]
        return [jnp.where(lane == 0, b, a) for a, b in zip(turned, [nothing] + turned[:-1])]

    def sweep(source, target, earlier, mask, degree):
        first = degree + 1

        def one_row(row, odd_row):
            sign = -even_sign if odd_row else even_sign
            second, onsite = SECOND_HOP * sign, ONSITE_MASS * sign
            down = odd_lane != odd_row
            factor = [mask[row, :, at] for at in tiles]
            halves = [[], []]
            for part in range(0, wide, 8):
                eight = slice(part, part + 8)
                far, rest = [], []
                for r in (0, 1):
                    centre = [source[row, r, eight, at] for at in tiles]
                    upper = [source[row + 1, r, eight, at] for at in tiles]
                    lower = [source[row - 1, r, eight, at] for at in tiles]
                    right, left = shift(centre, 1), shift(centre, -1)
                    both = [u + l for u, l in zip(upper, lower)]
                    if degree == 0:
                        ahead = shift([2.0 * v - w for v, w in zip(right, both)], 1)
                        behind = shift([2.0 * v - w for v, w in zip(left, both)], -1)
                        far.append([second * (v + w) for v, w in zip(ahead, behind)])
                        rest.append([v - w for v, w in zip(right, left)])
                    else:
                        ahead = shift([v - w for v, w in zip(right, both)], 1)
                        behind = shift([v - w for v, w in zip(left, both)], -1)
                        far.append([second * (v - w) for v, w in zip(ahead, behind)])
                        rest.append([
                            (onsite * c + jnp.where(down, l, u)) + (v + w)
                            for c, u, l, v, w in zip(centre, upper, lower, right, left)
                        ])
                if degree == 0:
                    applied = [
                        [-v - w for v, w in zip(rest[1], far[0])],
                        [v - w for v, w in zip(rest[0], far[1])],
                    ]
                else:
                    applied = [
                        [v - w for v, w in zip(rest[0], far[1])],
                        [v + w for v, w in zip(rest[1], far[0])],
                    ]
                for r in (0, 1):
                    results = [v * f for v, f in zip(applied[r], factor)]
                    if earlier is not None:
                        results = [v - earlier[row, r, eight, at] for v, at in zip(results, tiles)]
                    if target is not None:
                        for v, at in zip(results, tiles):
                            target[row, r, eight, at] = v
                    halves[r].append(results)
            for r in (0, 1):
                base = (r * MOM + degree) * wide
                for i, at in enumerate(tiles):
                    lanes = pl.ds(pl.multiple_of(row * width + at.start, LANES), LANES)
                    block = jnp.concatenate([half[i] for half in halves[r]], axis=0)
                    rounded[base : base + wide, lanes] = block.astype(jnp.bfloat16)

        def pair(step, carry):
            one_row(first + 2 * step, first % 2 == 1)
            one_row(first + 2 * step + 1, first % 2 == 0)
            return carry

        lax.fori_loop(0, (padded_rows - 2 * first) // 2, pair, 0)

    left_copy.wait()

    def widen(step, carry):
        at = pl.ds(pl.multiple_of(step * 16, 16), 16)
        block = left_held[at, :].astype(jnp.float32)
        for i, lanes in enumerate(tiles):
            left_wide[i, at, :] = block[:, lanes]
        return carry

    lax.fori_loop(0, left_ref.shape[0] // 16, widen, 0)
    left_count = left_ref.shape[0] // rows
    for row in range(rows):
        for i, lanes in enumerate(tiles):
            block = left_wide[i, pl.ds(row, left_count, stride=rows), :]
            left_flat[:, row * width + lanes.start : row * width + lanes.stop] = block.astype(jnp.bfloat16)

    def stage(chunk):
        held = arrived.at[chunk, pl.ds(HALO, rows)]
        pltpu.make_async_copy(held, held, piece_recv.at[chunk]).wait()
        for copy in rim_copies(chunk):
            copy.start()

    def compute(chunk):
        for copy in rim_copies(chunk):
            copy.wait()

        def mask_row(row, carry):
            for r in (0, 1):
                for part in range(0, wide, 8):
                    at = slice(part, part + 8)
                    for run in range(per_row):
                        lanes = slice(run * piece, (run + 1) * piece)
                        field0[row, r, at, lanes] = arrived[chunk, row, run, r, at, :] * present[row, :, lanes]
            return carry

        lax.fori_loop(0, padded_rows, mask_row, 0)
        sweep(field0, field1, None, present, 0)
        sweep(field1, field2, None, scaled, 1)
        sweep(field2, field3, field1, doubled, 2)
        sweep(field3, None, field2, doubled, 3)
        product = lax.dot_general(
            left_flat[...],
            rounded[:, HALO * width : (HALO + rows) * width],
            (((1,), (1,)), ((), ())),
            preferred_element_type=jnp.float32,
        )
        count_left = product.shape[0] // 2
        half = product.shape[1] // 2
        real, imaginary = product[:count_left], product[count_left:]
        swapped = pltpu.roll(imaginary, half, axis=1)
        wheres = lax.broadcasted_iota(jnp.int32, swapped.shape, 1)
        combined = real + jnp.where(wheres < half, swapped, -swapped)
        partial[pl.ds(pl.multiple_of(chunk * count_left, count_left), count_left), :] = combined

    def step_chunk(chunk, carry):
        @pl.when(chunk + 1 < chunks)
        def _():
            send_chunk(chunk + 1, 0)

        stage(chunk)
        compute(chunk)
        return carry

    lax.fori_loop(0, chunks, step_chunk, 0)

    share_rows = shares.shape[1]

    def rows_of(site):
        return pl.ds(pl.multiple_of(site * share_rows, share_rows), share_rows)

    def share_copy(step):
        site = lax.rem(my_site + step, sites)
        return pltpu.make_async_remote_copy(
            src_ref=partial.at[rows_of(site)],
            dst_ref=shares.at[my_site],
            send_sem=share_send.at[step],
            recv_sem=share_recv,
            device_id={"sites": site},
            device_id_type=MESH,
        )

    def total_copy(step):
        site = lax.rem(my_site + step, sites)
        return pltpu.make_async_remote_copy(
            src_ref=total.at[rows_of(my_site)],
            dst_ref=total.at[rows_of(my_site)],
            send_sem=total_send.at[step],
            recv_sem=total_recv,
            device_id={"sites": site},
            device_id_type=MESH,
        )

    def start_all(make, stop):
        def go(step, carry):
            make(step).start()
            return carry

        lax.fori_loop(1, stop, go, 0)

    def sent_all(make, stop):
        def go(step, carry):
            make(step).wait_send()
            return carry

        lax.fori_loop(1, stop, go, 0)

    start_all(share_copy, sites)
    pltpu.make_async_copy(partial.at[rows_of(my_site)], shares.at[my_site], share_recv).start()
    pltpu.make_async_copy(shares, shares, share_recv).wait()
    summed = shares[0]
    for site in range(1, sites):
        summed = summed + shares[site]
    total[rows_of(my_site), :] = summed
    start_all(total_copy, sites)
    whole = total.at[pl.ds(0, (sites - 1) * share_rows)]
    pltpu.make_async_copy(whole, whole, total_recv).wait()
    out_ref[...] = total[...]
    sent_all(share_copy, sites)
    sent_all(total_copy, sites)

    sent_all(functools.partial(piece_copy, chunks - 1), count)


def per_device_fused(groups, sites, right_vectors, left_vectors, vacancy):
    width_group, piece = right_vectors.shape[1], right_vectors.shape[5]
    count_left, rows, width = left_vectors.shape[1:]
    wide = COLS_AT_ONCE
    chunks = width_group // wide
    padded = rows + 2 * HALO
    field = pltpu.VMEM((padded, 2, wide, width), jnp.float32)
    mask = pltpu.VMEM((padded, 8, width), jnp.float32)
    sums = (chunks * count_left, 2 * MOM * wide)
    dma = pltpu.SemaphoreType.DMA
    call = pl.pallas_call(
        functools.partial(fused_kernel, groups, sites),
        out_shape=jax.ShapeDtypeStruct(sums, jnp.float32),
        in_specs=[
            pl.BlockSpec(memory_space=pltpu.HBM),
            pl.BlockSpec(memory_space=pltpu.HBM),
            pl.BlockSpec(memory_space=pltpu.VMEM),
        ],
        out_specs=pl.BlockSpec(memory_space=pltpu.VMEM),
        scratch_shapes=[
            pltpu.VMEM((chunks, padded, width // piece, 2, wide, piece), jnp.float32),
            field, field, field, field, mask, mask, mask,
            pltpu.VMEM((2 * MOM * wide, padded * width), jnp.bfloat16),
            pltpu.VMEM((chunks, groups * sites, 2, wide, piece), jnp.float32),
            pltpu.VMEM((2 * count_left * rows, width), jnp.bfloat16),
            pltpu.VMEM((width // LANES, 2 * count_left * rows, LANES), jnp.float32),
            pltpu.VMEM((2 * count_left, rows * width), jnp.bfloat16),
            pltpu.VMEM(sums, jnp.float32),
            pltpu.VMEM((sites, sums[0] // sites, sums[1]), jnp.float32),
            pltpu.VMEM(sums, jnp.float32),
            dma((chunks, groups * sites)), dma((chunks,)),
            dma((chunks, 2)), dma((chunks, 2)), dma((2,)), dma((2,)),
            dma((sites,)), dma, dma((sites,)), dma, dma, dma((chunks,)),
        ],
        compiler_params=pltpu.CompilerParams(
            collective_id=0, has_side_effects=True, vmem_limit_bytes=125 * 512 * 1024
        ),
        cost_estimate=pl.CostEstimate(flops=2 * 10**9, bytes_accessed=8 * 10**6, transcendentals=0),
    )
    summed = call(right_vectors, left_vectors.reshape(2 * count_left * rows, width), vacancy)
    summed = summed.reshape(chunks, count_left, 2, MOM, wide)
    return summed.transpose(2, 3, 1, 0, 4).reshape(2, MOM, count_left, width_group, 1)


def per_device(groups, sites, right_vectors, left_vectors, vacancy):
    columns, piece = right_vectors.shape[1], right_vectors.shape[5]
    count_left, rows, width = left_vectors.shape[1:]
    shares = (columns // COLS_AT_ONCE) * count_left
    fits = (
        piece % 128 == 0 and width % piece == 0 and right_vectors.shape[4] == 1
        and columns % COLS_AT_ONCE == 0 and rows % 2 == 0 and rows >= HALO
        and sites >= 4 and sites % 2 == 0 and shares % (8 * sites) == 0 and count_left % 8 == 0 and (2 * count_left * rows) % 16 == 0
    )
    if fits:
        return per_device_fused(groups, sites, right_vectors, left_vectors, vacancy)
    return per_device_plain(right_vectors, left_vectors, vacancy)


def solution(mesh):
    return jax.shard_map(
        functools.partial(per_device, mesh.shape["cols"], mesh.shape["sites"]),
        mesh=mesh,
        in_specs=(
            P(None, None, None, None, ("cols", "sites"), None),
            P(None, None, "sites", None),
            P("sites", None),
        ),
        out_specs=P(None, None, None, None, "cols"),
        check_vma=False,
    )
```

```python
import functools

import jax
import jax.numpy as jnp
from jax import lax
from jax.experimental import pallas as pl
from jax.experimental.pallas import tpu as pltpu
from jax.sharding import PartitionSpec as P

MOM = 4


ONSITE_MASS = 0.3
SECOND_HOP = 0.2
BAND_SCALE = 4.5


def padded_2(cells, sides, width):
    for axis, dim in sides:
        count = lax.axis_size(axis)
        head = lax.slice_in_dim(cells, 0, width, axis=dim)
        tail = lax.slice_in_dim(cells, cells.shape[dim] - width, cells.shape[dim], axis=dim)
        cells = jnp.concatenate(
            [
                lax.ppermute(tail, axis, [(i, (i + 1) % count) for i in range(count)]),
                cells,
                lax.ppermute(head, axis, [((i + 1) % count, i) for i in range(count)]),
            ],
            axis=dim,
        )
    return cells


def column_shift(values, offset):
    row_width = values.shape[-1]
    filler = jnp.zeros(values.shape[:-1] + (abs(offset),), values.dtype)
    if offset > 0:
        return jnp.concatenate([values[..., offset:], filler], axis=-1)
    return jnp.concatenate([filler, values[..., : row_width + offset]], axis=-1)


def rotate_phase(values):
    return jnp.stack([-values[1], values[0]])


def sign_table(row_count, row_width):
    rows_index = lax.broadcasted_iota(jnp.int32, (row_count, row_width), 0)
    cols_index = lax.broadcasted_iota(jnp.int32, (row_count, row_width), 1)
    return (1 - 2 * ((rows_index + cols_index) % 2)).astype(jnp.float32)


def haldane(padded, parity_sign):
    centre = padded[:, :, 1:-1, :]
    upper_row = padded[:, :, 2:, :]
    lower_row = padded[:, :, :-2, :]
    vertical = jnp.where(parity_sign > 0, upper_row, lower_row)
    nearest = column_shift(centre, 1) + column_shift(centre, -1) + vertical
    second = (
        column_shift(centre, 2)
        - column_shift(centre, -2)
        + column_shift(upper_row, -1)
        - column_shift(lower_row, 1)
        + column_shift(lower_row, -1)
        - column_shift(upper_row, 1)
    )
    return (
        ONSITE_MASS * parity_sign * centre
        + nearest
        + SECOND_HOP * parity_sign * rotate_phase(second)
    )


def velocity(padded, parity_sign):
    centre = padded[:, :, 1:-1, :]
    upper_row = padded[:, :, 2:, :]
    lower_row = padded[:, :, :-2, :]
    along_x = column_shift(centre, 1) - column_shift(centre, -1)
    farther = column_shift(centre, 2) + column_shift(centre, -2)
    diagonal = (
        column_shift(upper_row, 1)
        + column_shift(upper_row, -1)
        + column_shift(lower_row, 1)
        + column_shift(lower_row, -1)
    )
    return rotate_phase(along_x) - SECOND_HOP * parity_sign * (2.0 * farther - diagonal)


def with_rims(values):
    return padded_2(values, (("sites", 2),), 1)


def per_device_plain(right_vectors, left_vectors, vacancy):
    layout = right_vectors.shape
    pieces = right_vectors.reshape(layout[0], layout[1], layout[2], layout[3], layout[5])
    slab_field = lax.all_to_all(
        lax.all_to_all(pieces, "cols", split_axis=2, concat_axis=2, tiled=True),
        "sites",
        split_axis=3,
        concat_axis=3,
        tiled=True,
    )
    row_count = left_vectors.shape[2]
    row_width = left_vectors.shape[3]
    count_left = left_vectors.shape[1]
    group_width = layout[1]
    site_count = row_count * row_width
    present = vacancy.astype(jnp.float32)
    current = slab_field.reshape(2, group_width, row_count, row_width) * present
    parity_sign = sign_table(row_count, row_width)
    latest = velocity(with_rims(current), parity_sign) * present
    previous = latest
    moment_list = [latest]
    for degree in range(1, MOM):
        applied = haldane(with_rims(latest), parity_sign) * present / BAND_SCALE
        following = applied if degree == 1 else 2.0 * applied - previous
        previous, latest = (latest, following)
        moment_list.append(latest)
    left_matrix = left_vectors.reshape(2 * count_left, site_count)
    summed_list = []
    for moment in moment_list:
        rounded = moment.astype(jnp.bfloat16).reshape(2 * group_width, site_count)
        product = lax.dot_general(
            left_matrix, rounded, (((1,), (1,)), ((), ())), preferred_element_type=jnp.float32
        ).reshape(2, count_left, 2, group_width)
        combined = jnp.stack(
            [product[0, :, 0] + product[1, :, 1], product[0, :, 1] - product[1, :, 0]]
        )
        summed_list.append(lax.psum(combined, "sites"))
    summed = jnp.stack(summed_list, axis=1)
    return summed[..., None]


MESH = pl.DeviceIdType.MESH
HALO = MOM
COLS_AT_ONCE = 8
LANES = 128


def fused_kernel(
    groups, sites, right_ref, left_ref, vacancy_ref, out_ref,
    arrived, field0, field1, field2, field3, present, scaled, doubled, rounded,
    staged, left_held, left_wide, left_flat, partial, shares, total,
    piece_send, piece_recv, rim_send, rim_recv, mask_send, mask_recv,
    share_send, share_recv, total_send, total_recv, left_sem, stage_sem,
):
    chunks, padded_rows, per_row, _, wide, piece = arrived.shape
    width = per_row * piece
    rows = padded_rows - 2 * HALO
    count = groups * sites
    my_group, my_site = lax.axis_index("cols"), lax.axis_index("sites")
    mine = my_group * sites + my_site
    above, below = lax.rem(my_site + 1, sites), lax.rem(my_site + sites - 1, sites)

    def piece_of(chunk, group, site):
        return right_ref.at[:, pl.ds(pl.multiple_of(chunk * wide, wide), wide), group, site, 0, :]

    def lay_out(chunk, carry):
        def place(other, inner):
            pltpu.make_async_copy(
                piece_of(chunk, other // sites, lax.rem(other, sites)), staged.at[chunk, other], stage_sem.at[chunk]
            ).start()
            return inner

        lax.fori_loop(0, count, place, 0)
        return carry

    left_copy = pltpu.make_async_copy(left_ref, left_held, left_sem)
    left_copy.start()
    barrier = pltpu.get_barrier_semaphore()

    def greet(step, carry):
        other = lax.rem(mine + step, count)
        pl.semaphore_signal(
            barrier, inc=1, device_id={"cols": other // sites, "sites": lax.rem(other, sites)}, device_id_type=MESH
        )
        return carry

    lax.fori_loop(1, count, greet, 0)
    lay_out(0, 0)

    for row in range(rows):
        present[HALO + row] = jnp.broadcast_to(vacancy_ref[row : row + 1, :].astype(jnp.float32), (8, width))

    pl.semaphore_wait(barrier, count - 1)

    def landing(chunk, run):
        return arrived.at[chunk, HALO + run // per_row, lax.rem(run, per_row)]

    def piece_copy(chunk, step):
        turn = lax.rem(step, 2) * (sites // 2) + step // (2 * groups)
        group = lax.rem(my_group + lax.rem(step // 2, groups), groups)
        site = lax.rem(my_site + turn, sites)
        return pltpu.make_async_remote_copy(
            src_ref=staged.at[chunk, group * sites + site],
            dst_ref=landing(chunk, mine),
            send_sem=piece_send.at[chunk, step],
            recv_sem=piece_recv.at[chunk],
            device_id={"cols": group, "sites": site},
            device_id_type=MESH,
        )

    def rim_copy(source, send_sem, recv_sem, up):
        first = rows if up else HALO
        landing_row = 0 if up else rows + HALO
        return pltpu.make_async_remote_copy(
            src_ref=source.at[pl.ds(first, HALO)],
            dst_ref=source.at[pl.ds(landing_row, HALO)],
            send_sem=send_sem,
            recv_sem=recv_sem,
            device_id={"sites": above if up else below},
            device_id_type=MESH,
        )

    def mask_copies():
        return [rim_copy(present, mask_send.at[i], mask_recv.at[i], up) for i, up in enumerate((True, False))]

    def rim_copies(chunk):
        return [
            rim_copy(arrived.at[chunk], rim_send.at[chunk, i], rim_recv.at[chunk, i], up)
            for i, up in enumerate((True, False))
        ]

    for copy in mask_copies():
        copy.start()

    def send_chunk(chunk, carry):
        pltpu.make_async_copy(staged.at[chunk], staged.at[chunk], stage_sem.at[chunk]).wait()

        def send(step, inner):
            piece_copy(chunk, step).start()
            return inner

        lax.fori_loop(1, count, send, 0)
        pltpu.make_async_copy(staged.at[chunk, mine], landing(chunk, mine), piece_recv.at[chunk]).start()
        return carry

    send_chunk(0, 0)
    lax.fori_loop(1, chunks, lay_out, 0)
    lax.fori_loop(1, min(2, chunks), send_chunk, 0)

    for copy in mask_copies():
        copy.wait()

    def scale_masks(row, carry):
        held = present[row]
        scaled[row] = held * (1.0 / BAND_SCALE)
        doubled[row] = held * (2.0 / BAND_SCALE)
        return carry

    lax.fori_loop(0, padded_rows, scale_masks, 0)

    tiles = [slice(at, at + LANES) for at in range(0, width, LANES)]
    lane = lax.broadcasted_iota(jnp.int32, (8, LANES), 1)
    odd_lane = lax.rem(lane, 2) == 1
    even_sign = jnp.where(odd_lane, -1.0, 1.0)
    nothing = jnp.zeros((8, LANES), jnp.float32)

    def shift(values, offset):
        if offset > 0:
            turned = [pltpu.roll(v, LANES - 1, axis=1) for v in values]
            return [jnp.where(lane == LANES - 1, b, a) for a, b in zip(turned, turned[1:] + [nothing])]
        turned = [pltpu.roll(v, 1, axis=1) for v in values]
        return [jnp.where(lane == 0, b, a) for a, b in zip(turned, [nothing] + turned[:-1])]

    def sweep(chunk, source, target, earlier, mask, degree):
        first = degree + 1

        base = pl.multiple_of(lax.rem(chunk, 2) * 2 * MOM * wide + degree * 2 * wide, 2 * wide)

        def one_row(row, odd_row):
            sign = -even_sign if odd_row else even_sign
            second, onsite = SECOND_HOP * sign, ONSITE_MASS * sign
            down = odd_lane != odd_row
            factor = [mask[row, :, at] for at in tiles]
            parts = []
            for part in range(0, wide, 8):
                eight = slice(part, part + 8)
                far, rest = [], []
                for r in (0, 1):
                    centre = [source[row, r, eight, at] for at in tiles]
                    upper = [source[row + 1, r, eight, at] for at in tiles]
                    lower = [source[row - 1, r, eight, at] for at in tiles]
                    right, left = shift(centre, 1), shift(centre, -1)
                    both = [u + l for u, l in zip(upper, lower)]
                    if degree == 0:
                        ahead = shift([2.0 * v - w for v, w in zip(right, both)], 1)
                        behind = shift([2.0 * v - w for v, w in zip(left, both)], -1)
                        far.append([second * (v + w) for v, w in zip(ahead, behind)])
                        rest.append([v - w for v, w in zip(right, left)])
                    else:
                        ahead = shift([v - w for v, w in zip(right, both)], 1)
                        behind = shift([v - w for v, w in zip(left, both)], -1)
                        far.append([second * (v - w) for v, w in zip(ahead, behind)])
                        rest.append([
                            (onsite * c + jnp.where(down, l, u)) + (v + w)
                            for c, u, l, v, w in zip(centre, upper, lower, right, left)
                        ])
                if degree == 0:
                    applied = [
                        [-v - w for v, w in zip(rest[1], far[0])],
                        [v - w for v, w in zip(rest[0], far[1])],
                    ]
                else:
                    applied = [
                        [v - w for v, w in zip(rest[0], far[1])],
                        [v + w for v, w in zip(rest[1], far[0])],
                    ]
                for r in (0, 1):
                    results = [v * f for v, f in zip(applied[r], factor)]
                    if earlier is not None:
                        results = [v - earlier[row, r, eight, at] for v, at in zip(results, tiles)]
                    if target is not None:
                        for v, at in zip(results, tiles):
                            target[row, r, eight, at] = v
                    parts.append(results)
            for i, at in enumerate(tiles):
                lanes = pl.ds(pl.multiple_of(row * width + at.start, LANES), LANES)
                block = jnp.concatenate([part[i] for part in parts], axis=0)
                rounded[pl.ds(base, 2 * wide), lanes] = block.astype(jnp.bfloat16)

        def pair(step, carry):
            one_row(first + 2 * step, first % 2 == 1)
            one_row(first + 2 * step + 1, first % 2 == 0)
            return carry

        lax.fori_loop(0, (padded_rows - 2 * first) // 2, pair, 0)

    left_copy.wait()

    def widen(step, carry):
        at = pl.ds(pl.multiple_of(step * 16, 16), 16)
        block = left_held[at, :].astype(jnp.float32)
        for i, lanes in enumerate(tiles):
            left_wide[i, at, :] = block[:, lanes]
        return carry

    lax.fori_loop(0, left_ref.shape[0] // 16, widen, 0)
    left_count = left_ref.shape[0] // rows
    for row in range(rows):
        for i, lanes in enumerate(tiles):
            block = left_wide[i, pl.ds(row, left_count, stride=rows), :]
            left_flat[:, row * width + lanes.start : row * width + lanes.stop] = block.astype(jnp.bfloat16)

    def stage(chunk):
        held = arrived.at[chunk, pl.ds(HALO, rows)]
        pltpu.make_async_copy(held, held, piece_recv.at[chunk]).wait()
        for copy in rim_copies(chunk):
            copy.start()

        @pl.when(chunk + 2 < chunks)
        def _():
            send_chunk(chunk + 2, 0)

    def compute(chunk):
        for copy in rim_copies(chunk):
            copy.wait()

        def mask_row(row, carry):
            for r in (0, 1):
                for part in range(0, wide, 8):
                    at = slice(part, part + 8)
                    for run in range(per_row):
                        lanes = slice(run * piece, (run + 1) * piece)
                        field0[row, r, at, lanes] = arrived[chunk, row, run, r, at, :] * present[row, :, lanes]
            return carry

        lax.fori_loop(0, padded_rows, mask_row, 0)
        sweep(chunk, field0, field1, None, present, 0)
        sweep(chunk, field1, field2, None, scaled, 1)
        sweep(chunk, field2, field3, field1, doubled, 2)
        sweep(chunk, field3, None, field2, doubled, 3)

        @pl.when(lax.rem(chunk, 2) == 1)
        def _():
            multiply(chunk // 2)

    def multiply(couple):
        product = lax.dot_general(
            left_flat[...],
            rounded[:, HALO * width : (HALO + rows) * width],
            (((1,), (1,)), ((), ())),
            preferred_element_type=jnp.float32,
        )
        count_left = product.shape[0] // 2
        real, imaginary = product[:count_left], product[count_left:]
        last = lax.rem(lax.broadcasted_iota(jnp.int32, imaginary.shape, 1), 2 * wide) >= wide
        ahead = pltpu.roll(imaginary, imaginary.shape[1] - wide, axis=1)
        behind = pltpu.roll(imaginary, wide, axis=1)
        combined = real + jnp.where(last, -behind, ahead)
        partial[pl.ds(pl.multiple_of(couple * count_left, count_left), count_left), :] = combined

    def step_chunk(step, carry):
        @pl.when(step < chunks)
        def _():
            stage(step)

        @pl.when(step > 0)
        def _():
            compute(step - 1)

        return carry

    lax.fori_loop(0, chunks + 1, step_chunk, 0)

    share_rows = shares.shape[1]

    def rows_of(site):
        return pl.ds(pl.multiple_of(site * share_rows, share_rows), share_rows)

    def share_copy(step):
        site = lax.rem(my_site + step, sites)
        return pltpu.make_async_remote_copy(
            src_ref=partial.at[rows_of(site)],
            dst_ref=shares.at[my_site],
            send_sem=share_send.at[step],
            recv_sem=share_recv,
            device_id={"sites": site},
            device_id_type=MESH,
        )

    def total_copy(step):
        site = lax.rem(my_site + step, sites)
        return pltpu.make_async_remote_copy(
            src_ref=total.at[rows_of(my_site)],
            dst_ref=total.at[rows_of(my_site)],
            send_sem=total_send.at[step],
            recv_sem=total_recv,
            device_id={"sites": site},
            device_id_type=MESH,
        )

    def start_all(make, stop):
        def go(step, carry):
            make(step).start()
            return carry

        lax.fori_loop(1, stop, go, 0)

    def sent_all(make, stop):
        def go(step, carry):
            make(step).wait_send()
            return carry

        lax.fori_loop(1, stop, go, 0)

    start_all(share_copy, sites)
    pltpu.make_async_copy(partial.at[rows_of(my_site)], shares.at[my_site], share_recv).start()
    pltpu.make_async_copy(shares, shares, share_recv).wait()
    summed = shares[0]
    for site in range(1, sites):
        summed = summed + shares[site]
    total[rows_of(my_site), :] = summed
    start_all(total_copy, sites)
    whole = total.at[pl.ds(0, (sites - 1) * share_rows)]
    pltpu.make_async_copy(whole, whole, total_recv).wait()
    out_ref[...] = total[...]
    sent_all(share_copy, sites)
    sent_all(total_copy, sites)

    def sent_chunk(chunk, carry):
        sent_all(functools.partial(piece_copy, chunk), count)
        return carry

    lax.fori_loop(0, chunks, sent_chunk, 0)


def per_device_fused(groups, sites, right_vectors, left_vectors, vacancy):
    width_group, piece = right_vectors.shape[1], right_vectors.shape[5]
    count_left, rows, width = left_vectors.shape[1:]
    wide = COLS_AT_ONCE
    chunks = width_group // wide
    padded = rows + 2 * HALO
    field = pltpu.VMEM((padded, 2, wide, width), jnp.float32)
    mask = pltpu.VMEM((padded, 8, width), jnp.float32)
    sums = (chunks // 2 * count_left, 4 * MOM * wide)
    dma = pltpu.SemaphoreType.DMA
    call = pl.pallas_call(
        functools.partial(fused_kernel, groups, sites),
        out_shape=jax.ShapeDtypeStruct(sums, jnp.float32),
        in_specs=[
            pl.BlockSpec(memory_space=pltpu.HBM),
            pl.BlockSpec(memory_space=pltpu.HBM),
            pl.BlockSpec(memory_space=pltpu.VMEM),
        ],
        out_specs=pl.BlockSpec(memory_space=pltpu.VMEM),
        scratch_shapes=[
            pltpu.VMEM((chunks, padded, width // piece, 2, wide, piece), jnp.float32),
            field, field, field, field, mask, mask, mask,
            pltpu.VMEM((4 * MOM * wide, padded * width), jnp.bfloat16),
            pltpu.VMEM((chunks, groups * sites, 2, wide, piece), jnp.float32),
            pltpu.VMEM((2 * count_left * rows, width), jnp.bfloat16),
            pltpu.VMEM((width // LANES, 2 * count_left * rows, LANES), jnp.float32),
            pltpu.VMEM((2 * count_left, rows * width), jnp.bfloat16),
            pltpu.VMEM(sums, jnp.float32),
            pltpu.VMEM((sites, sums[0] // sites, sums[1]), jnp.float32),
            pltpu.VMEM(sums, jnp.float32),
            dma((chunks, groups * sites)), dma((chunks,)),
            dma((chunks, 2)), dma((chunks, 2)), dma((2,)), dma((2,)),
            dma((sites,)), dma, dma((sites,)), dma, dma, dma((chunks,)),
        ],
        compiler_params=pltpu.CompilerParams(
            collective_id=0, has_side_effects=True, vmem_limit_bytes=125 * 512 * 1024
        ),
        cost_estimate=pl.CostEstimate(flops=2 * 10**9, bytes_accessed=8 * 10**6, transcendentals=0),
    )
    summed = call(right_vectors, left_vectors.reshape(2 * count_left * rows, width), vacancy)
    summed = summed.reshape(chunks // 2, count_left, 2, MOM, 2, wide)
    return summed.transpose(4, 3, 1, 0, 2, 5).reshape(2, MOM, count_left, width_group, 1)


def per_device(groups, sites, right_vectors, left_vectors, vacancy):
    columns, piece = right_vectors.shape[1], right_vectors.shape[5]
    count_left, rows, width = left_vectors.shape[1:]
    shares = columns // (2 * COLS_AT_ONCE) * count_left
    fits = (
        piece % 128 == 0 and width % piece == 0 and right_vectors.shape[4] == 1
        and columns % (2 * COLS_AT_ONCE) == 0 and rows % 2 == 0 and rows >= HALO
        and sites >= 4 and sites % 2 == 0 and shares % (8 * sites) == 0 and count_left % 8 == 0 and (2 * count_left * rows) % 16 == 0
    )
    if fits:
        return per_device_fused(groups, sites, right_vectors, left_vectors, vacancy)
    return per_device_plain(right_vectors, left_vectors, vacancy)


def solution(mesh):
    return jax.shard_map(
        functools.partial(per_device, mesh.shape["cols"], mesh.shape["sites"]),
        mesh=mesh,
        in_specs=(
            P(None, None, None, None, ("cols", "sites"), None),
            P(None, None, "sites", None),
            P("sites", None),
        ),
        out_specs=P(None, None, None, None, "cols"),
        check_vma=False,
    )
```

```python
import functools

import jax
import jax.numpy as jnp
from jax import lax
from jax.experimental import pallas as pl
from jax.experimental.pallas import tpu as pltpu
from jax.sharding import PartitionSpec as P

MOM = 4


ONSITE_MASS = 0.3
SECOND_HOP = 0.2
BAND_SCALE = 4.5


def padded_2(cells, sides, width):
    for axis, dim in sides:
        count = lax.axis_size(axis)
        head = lax.slice_in_dim(cells, 0, width, axis=dim)
        tail = lax.slice_in_dim(cells, cells.shape[dim] - width, cells.shape[dim], axis=dim)
        cells = jnp.concatenate(
            [
                lax.ppermute(tail, axis, [(i, (i + 1) % count) for i in range(count)]),
                cells,
                lax.ppermute(head, axis, [((i + 1) % count, i) for i in range(count)]),
            ],
            axis=dim,
        )
    return cells


def column_shift(values, offset):
    row_width = values.shape[-1]
    filler = jnp.zeros(values.shape[:-1] + (abs(offset),), values.dtype)
    if offset > 0:
        return jnp.concatenate([values[..., offset:], filler], axis=-1)
    return jnp.concatenate([filler, values[..., : row_width + offset]], axis=-1)


def rotate_phase(values):
    return jnp.stack([-values[1], values[0]])


def sign_table(row_count, row_width):
    rows_index = lax.broadcasted_iota(jnp.int32, (row_count, row_width), 0)
    cols_index = lax.broadcasted_iota(jnp.int32, (row_count, row_width), 1)
    return (1 - 2 * ((rows_index + cols_index) % 2)).astype(jnp.float32)


def haldane(padded, parity_sign):
    centre = padded[:, :, 1:-1, :]
    upper_row = padded[:, :, 2:, :]
    lower_row = padded[:, :, :-2, :]
    vertical = jnp.where(parity_sign > 0, upper_row, lower_row)
    nearest = column_shift(centre, 1) + column_shift(centre, -1) + vertical
    second = (
        column_shift(centre, 2)
        - column_shift(centre, -2)
        + column_shift(upper_row, -1)
        - column_shift(lower_row, 1)
        + column_shift(lower_row, -1)
        - column_shift(upper_row, 1)
    )
    return (
        ONSITE_MASS * parity_sign * centre
        + nearest
        + SECOND_HOP * parity_sign * rotate_phase(second)
    )


def velocity(padded, parity_sign):
    centre = padded[:, :, 1:-1, :]
    upper_row = padded[:, :, 2:, :]
    lower_row = padded[:, :, :-2, :]
    along_x = column_shift(centre, 1) - column_shift(centre, -1)
    farther = column_shift(centre, 2) + column_shift(centre, -2)
    diagonal = (
        column_shift(upper_row, 1)
        + column_shift(upper_row, -1)
        + column_shift(lower_row, 1)
        + column_shift(lower_row, -1)
    )
    return rotate_phase(along_x) - SECOND_HOP * parity_sign * (2.0 * farther - diagonal)


def with_rims(values):
    return padded_2(values, (("sites", 2),), 1)


def per_device_plain(right_vectors, left_vectors, vacancy):
    layout = right_vectors.shape
    pieces = right_vectors.reshape(layout[0], layout[1], layout[2], layout[3], layout[5])
    slab_field = lax.all_to_all(
        lax.all_to_all(pieces, "cols", split_axis=2, concat_axis=2, tiled=True),
        "sites",
        split_axis=3,
        concat_axis=3,
        tiled=True,
    )
    row_count = left_vectors.shape[2]
    row_width = left_vectors.shape[3]
    count_left = left_vectors.shape[1]
    group_width = layout[1]
    site_count = row_count * row_width
    present = vacancy.astype(jnp.float32)
    current = slab_field.reshape(2, group_width, row_count, row_width) * present
    parity_sign = sign_table(row_count, row_width)
    latest = velocity(with_rims(current), parity_sign) * present
    previous = latest
    moment_list = [latest]
    for degree in range(1, MOM):
        applied = haldane(with_rims(latest), parity_sign) * present / BAND_SCALE
        following = applied if degree == 1 else 2.0 * applied - previous
        previous, latest = (latest, following)
        moment_list.append(latest)
    left_matrix = left_vectors.reshape(2 * count_left, site_count)
    summed_list = []
    for moment in moment_list:
        rounded = moment.astype(jnp.bfloat16).reshape(2 * group_width, site_count)
        product = lax.dot_general(
            left_matrix, rounded, (((1,), (1,)), ((), ())), preferred_element_type=jnp.float32
        ).reshape(2, count_left, 2, group_width)
        combined = jnp.stack(
            [product[0, :, 0] + product[1, :, 1], product[0, :, 1] - product[1, :, 0]]
        )
        summed_list.append(lax.psum(combined, "sites"))
    summed = jnp.stack(summed_list, axis=1)
    return summed[..., None]


MESH = pl.DeviceIdType.MESH
HALO = MOM
COLS_AT_ONCE = 8
LANES = 128
IN_FLIGHT = 3


def fused_kernel(
    groups, sites, right_ref, left_ref, vacancy_ref, out_ref,
    arrived, field0, field1, field2, field3, present, scaled, doubled, rounded,
    staged, left_held, left_wide, left_flat, partial, shares, total,
    piece_send, piece_recv, rim_send, rim_recv, mask_send, mask_recv,
    share_send, share_recv, total_send, total_recv, left_sem, stage_sem,
):
    chunks, padded_rows, per_row, _, wide, piece = arrived.shape
    width = per_row * piece
    rows = padded_rows - 2 * HALO
    count = groups * sites
    my_group, my_site = lax.axis_index("cols"), lax.axis_index("sites")
    mine = my_group * sites + my_site
    above, below = lax.rem(my_site + 1, sites), lax.rem(my_site + sites - 1, sites)

    def piece_of(chunk, group, site):
        return right_ref.at[:, pl.ds(pl.multiple_of(chunk * wide, wide), wide), group, site, 0, :]

    def lay_out(chunk, carry):
        def place(other, inner):
            pltpu.make_async_copy(
                piece_of(chunk, other // sites, lax.rem(other, sites)), staged.at[chunk, other], stage_sem.at[chunk]
            ).start()
            return inner

        lax.fori_loop(0, count, place, 0)
        return carry

    left_copy = pltpu.make_async_copy(left_ref, left_held, left_sem)
    left_copy.start()
    barrier = pltpu.get_barrier_semaphore()

    def greet(step, carry):
        other = lax.rem(mine + step, count)
        pl.semaphore_signal(
            barrier, inc=1, device_id={"cols": other // sites, "sites": lax.rem(other, sites)}, device_id_type=MESH
        )
        return carry

    lax.fori_loop(1, count, greet, 0)
    lay_out(0, 0)

    for row in range(rows):
        present[HALO + row] = jnp.broadcast_to(vacancy_ref[row : row + 1, :].astype(jnp.float32), (8, width))

    pl.semaphore_wait(barrier, count - 1)

    def landing(chunk, run):
        return arrived.at[chunk, HALO + run // per_row, lax.rem(run, per_row)]

    def piece_copy(chunk, step):
        turn = lax.rem(step, 2) * (sites // 2) + step // (2 * groups)
        group = lax.rem(my_group + lax.rem(step // 2, groups), groups)
        site = lax.rem(my_site + turn, sites)
        return pltpu.make_async_remote_copy(
            src_ref=staged.at[chunk, group * sites + site],
            dst_ref=landing(chunk, mine),
            send_sem=piece_send.at[chunk, step],
            recv_sem=piece_recv.at[chunk],
            device_id={"cols": group, "sites": site},
            device_id_type=MESH,
        )

    def rim_copy(source, send_sem, recv_sem, up):
        first = rows if up else HALO
        landing_row = 0 if up else rows + HALO
        return pltpu.make_async_remote_copy(
            src_ref=source.at[pl.ds(first, HALO)],
            dst_ref=source.at[pl.ds(landing_row, HALO)],
            send_sem=send_sem,
            recv_sem=recv_sem,
            device_id={"sites": above if up else below},
            device_id_type=MESH,
        )

    def mask_copies():
        return [rim_copy(present, mask_send.at[i], mask_recv.at[i], up) for i, up in enumerate((True, False))]

    def rim_copies(chunk):
        return [
            rim_copy(arrived.at[chunk], rim_send.at[chunk, i], rim_recv.at[chunk, i], up)
            for i, up in enumerate((True, False))
        ]

    for copy in mask_copies():
        copy.start()

    def send_chunk(chunk, carry):
        pltpu.make_async_copy(staged.at[chunk], staged.at[chunk], stage_sem.at[chunk]).wait()

        def send(step, inner):
            piece_copy(chunk, step).start()
            return inner

        lax.fori_loop(1, count, send, 0)
        pltpu.make_async_copy(staged.at[chunk, mine], landing(chunk, mine), piece_recv.at[chunk]).start()
        return carry

    send_chunk(0, 0)
    lax.fori_loop(1, chunks, lay_out, 0)
    lax.fori_loop(1, min(IN_FLIGHT, chunks), send_chunk, 0)

    for copy in mask_copies():
        copy.wait()

    def scale_masks(row, carry):
        held = present[row]
        scaled[row] = held * (1.0 / BAND_SCALE)
        doubled[row] = held * (2.0 / BAND_SCALE)
        return carry

    lax.fori_loop(0, padded_rows, scale_masks, 0)

    tiles = [slice(at, at + LANES) for at in range(0, width, LANES)]
    lane = lax.broadcasted_iota(jnp.int32, (8, LANES), 1)
    odd_lane = lax.rem(lane, 2) == 1
    even_sign = jnp.where(odd_lane, -1.0, 1.0)
    nothing = jnp.zeros((8, LANES), jnp.float32)

    def shift(values, offset):
        if offset > 0:
            turned = [pltpu.roll(v, LANES - 1, axis=1) for v in values]
            return [jnp.where(lane == LANES - 1, b, a) for a, b in zip(turned, turned[1:] + [nothing])]
        turned = [pltpu.roll(v, 1, axis=1) for v in values]
        return [jnp.where(lane == 0, b, a) for a, b in zip(turned, [nothing] + turned[:-1])]

    def sweep(chunk, source, target, earlier, mask, degree):
        first = degree + 1

        base = pl.multiple_of(lax.rem(chunk, 2) * 2 * MOM * wide + degree * 2 * wide, 2 * wide)

        def one_row(row, odd_row):
            sign = -even_sign if odd_row else even_sign
            second, onsite = SECOND_HOP * sign, ONSITE_MASS * sign
            down = odd_lane != odd_row
            factor = [mask[row, :, at] for at in tiles]
            parts = []
            for part in range(0, wide, 8):
                eight = slice(part, part + 8)
                far, rest = [], []
                for r in (0, 1):
                    centre = [source[row, r, eight, at] for at in tiles]
                    upper = [source[row + 1, r, eight, at] for at in tiles]
                    lower = [source[row - 1, r, eight, at] for at in tiles]
                    right, left = shift(centre, 1), shift(centre, -1)
                    both = [u + l for u, l in zip(upper, lower)]
                    if degree == 0:
                        ahead = shift([2.0 * v - w for v, w in zip(right, both)], 1)
                        behind = shift([2.0 * v - w for v, w in zip(left, both)], -1)
                        far.append([second * (v + w) for v, w in zip(ahead, behind)])
                        rest.append([v - w for v, w in zip(right, left)])
                    else:
                        ahead = shift([v - w for v, w in zip(right, both)], 1)
                        behind = shift([v - w for v, w in zip(left, both)], -1)
                        far.append([second * (v - w) for v, w in zip(ahead, behind)])
                        rest.append([
                            (onsite * c + jnp.where(down, l, u)) + (v + w)
                            for c, u, l, v, w in zip(centre, upper, lower, right, left)
                        ])
                if degree == 0:
                    applied = [
                        [-v - w for v, w in zip(rest[1], far[0])],
                        [v - w for v, w in zip(rest[0], far[1])],
                    ]
                else:
                    applied = [
                        [v - w for v, w in zip(rest[0], far[1])],
                        [v + w for v, w in zip(rest[1], far[0])],
                    ]
                for r in (0, 1):
                    results = [v * f for v, f in zip(applied[r], factor)]
                    if earlier is not None:
                        results = [v - earlier[row, r, eight, at] for v, at in zip(results, tiles)]
                    if target is not None:
                        for v, at in zip(results, tiles):
                            target[row, r, eight, at] = v
                    parts.append(results)
            for i, at in enumerate(tiles):
                lanes = pl.ds(pl.multiple_of(row * width + at.start, LANES), LANES)
                block = jnp.concatenate([part[i] for part in parts], axis=0)
                rounded[pl.ds(base, 2 * wide), lanes] = block.astype(jnp.bfloat16)

        def pair(step, carry):
            one_row(first + 2 * step, first % 2 == 1)
            one_row(first + 2 * step + 1, first % 2 == 0)
            return carry

        lax.fori_loop(0, (padded_rows - 2 * first) // 2, pair, 0)

    left_copy.wait()

    def widen(step, carry):
        at = pl.ds(pl.multiple_of(step * 16, 16), 16)
        block = left_held[at, :].astype(jnp.float32)
        for i, lanes in enumerate(tiles):
            left_wide[i, at, :] = block[:, lanes]
        return carry

    lax.fori_loop(0, left_ref.shape[0] // 16, widen, 0)
    left_count = left_ref.shape[0] // rows
    for row in range(rows):
        for i, lanes in enumerate(tiles):
            block = left_wide[i, pl.ds(row, left_count, stride=rows), :]
            left_flat[:, row * width + lanes.start : row * width + lanes.stop] = block.astype(jnp.bfloat16)

    def stage(chunk):
        held = arrived.at[chunk, pl.ds(HALO, rows)]
        pltpu.make_async_copy(held, held, piece_recv.at[chunk]).wait()
        for copy in rim_copies(chunk):
            copy.start()

        @pl.when(chunk + IN_FLIGHT < chunks)
        def _():
            send_chunk(chunk + IN_FLIGHT, 0)

    def compute(chunk):
        for copy in rim_copies(chunk):
            copy.wait()

        def mask_row(row, carry):
            for r in (0, 1):
                for part in range(0, wide, 8):
                    at = slice(part, part + 8)
                    for run in range(per_row):
                        lanes = slice(run * piece, (run + 1) * piece)
                        field0[row, r, at, lanes] = arrived[chunk, row, run, r, at, :] * present[row, :, lanes]
            return carry

        lax.fori_loop(0, padded_rows, mask_row, 0)
        sweep(chunk, field0, field1, None, present, 0)
        sweep(chunk, field1, field2, None, scaled, 1)
        sweep(chunk, field2, field3, field1, doubled, 2)
        sweep(chunk, field3, None, field2, doubled, 3)

        @pl.when(lax.rem(chunk, 2) == 1)
        def _():
            multiply(chunk // 2)

    def multiply(couple):
        product = lax.dot_general(
            left_flat[...],
            rounded[:, HALO * width : (HALO + rows) * width],
            (((1,), (1,)), ((), ())),
            preferred_element_type=jnp.float32,
        )
        count_left = product.shape[0] // 2
        real, imaginary = product[:count_left], product[count_left:]
        last = lax.rem(lax.broadcasted_iota(jnp.int32, imaginary.shape, 1), 2 * wide) >= wide
        ahead = pltpu.roll(imaginary, imaginary.shape[1] - wide, axis=1)
        behind = pltpu.roll(imaginary, wide, axis=1)
        combined = real + jnp.where(last, -behind, ahead)
        partial[pl.ds(pl.multiple_of(couple * count_left, count_left), count_left), :] = combined

    def step_chunk(step, carry):
        @pl.when(step < chunks)
        def _():
            stage(step)

        @pl.when(step > 0)
        def _():
            compute(step - 1)

        return carry

    lax.fori_loop(0, chunks + 1, step_chunk, 0)

    share_rows = shares.shape[1]

    def rows_of(site):
        return pl.ds(pl.multiple_of(site * share_rows, share_rows), share_rows)

    def share_copy(step):
        site = lax.rem(my_site + step, sites)
        return pltpu.make_async_remote_copy(
            src_ref=partial.at[rows_of(site)],
            dst_ref=shares.at[my_site],
            send_sem=share_send.at[step],
            recv_sem=share_recv,
            device_id={"sites": site},
            device_id_type=MESH,
        )

    def total_copy(step):
        site = lax.rem(my_site + step, sites)
        return pltpu.make_async_remote_copy(
            src_ref=total.at[rows_of(my_site)],
            dst_ref=total.at[rows_of(my_site)],
            send_sem=total_send.at[step],
            recv_sem=total_recv,
            device_id={"sites": site},
            device_id_type=MESH,
        )

    def start_all(make, stop):
        def go(step, carry):
            make(step).start()
            return carry

        lax.fori_loop(1, stop, go, 0)

    def sent_all(make, stop):
        def go(step, carry):
            make(step).wait_send()
            return carry

        lax.fori_loop(1, stop, go, 0)

    start_all(share_copy, sites)
    pltpu.make_async_copy(partial.at[rows_of(my_site)], shares.at[my_site], share_recv).start()
    pltpu.make_async_copy(shares, shares, share_recv).wait()
    summed = shares[0]
    for site in range(1, sites):
        summed = summed + shares[site]
    total[rows_of(my_site), :] = summed
    start_all(total_copy, sites)
    whole = total.at[pl.ds(0, (sites - 1) * share_rows)]
    pltpu.make_async_copy(whole, whole, total_recv).wait()
    out_ref[...] = total[...]
    sent_all(share_copy, sites)
    sent_all(total_copy, sites)

    def sent_chunk(chunk, carry):
        sent_all(functools.partial(piece_copy, chunk), count)
        return carry

    lax.fori_loop(0, chunks, sent_chunk, 0)


def per_device_fused(groups, sites, right_vectors, left_vectors, vacancy):
    width_group, piece = right_vectors.shape[1], right_vectors.shape[5]
    count_left, rows, width = left_vectors.shape[1:]
    wide = COLS_AT_ONCE
    chunks = width_group // wide
    padded = rows + 2 * HALO
    field = pltpu.VMEM((padded, 2, wide, width), jnp.float32)
    mask = pltpu.VMEM((padded, 8, width), jnp.float32)
    sums = (chunks // 2 * count_left, 4 * MOM * wide)
    dma = pltpu.SemaphoreType.DMA
    call = pl.pallas_call(
        functools.partial(fused_kernel, groups, sites),
        out_shape=jax.ShapeDtypeStruct(sums, jnp.float32),
        in_specs=[
            pl.BlockSpec(memory_space=pltpu.HBM),
            pl.BlockSpec(memory_space=pltpu.HBM),
            pl.BlockSpec(memory_space=pltpu.VMEM),
        ],
        out_specs=pl.BlockSpec(memory_space=pltpu.VMEM),
        scratch_shapes=[
            pltpu.VMEM((chunks, padded, width // piece, 2, wide, piece), jnp.float32),
            field, field, field, field, mask, mask, mask,
            pltpu.VMEM((4 * MOM * wide, padded * width), jnp.bfloat16),
            pltpu.VMEM((chunks, groups * sites, 2, wide, piece), jnp.float32),
            pltpu.VMEM((2 * count_left * rows, width), jnp.bfloat16),
            pltpu.VMEM((width // LANES, 2 * count_left * rows, LANES), jnp.float32),
            pltpu.VMEM((2 * count_left, rows * width), jnp.bfloat16),
            pltpu.VMEM(sums, jnp.float32),
            pltpu.VMEM((sites, sums[0] // sites, sums[1]), jnp.float32),
            pltpu.VMEM(sums, jnp.float32),
            dma((chunks, groups * sites)), dma((chunks,)),
            dma((chunks, 2)), dma((chunks, 2)), dma((2,)), dma((2,)),
            dma((sites,)), dma, dma((sites,)), dma, dma, dma((chunks,)),
        ],
        compiler_params=pltpu.CompilerParams(
            collective_id=0, has_side_effects=True, vmem_limit_bytes=125 * 512 * 1024
        ),
        cost_estimate=pl.CostEstimate(flops=2 * 10**9, bytes_accessed=8 * 10**6, transcendentals=0),
    )
    summed = call(right_vectors, left_vectors.reshape(2 * count_left * rows, width), vacancy)
    summed = summed.reshape(chunks // 2, count_left, 2, MOM, 2, wide)
    return summed.transpose(4, 3, 1, 0, 2, 5).reshape(2, MOM, count_left, width_group, 1)


def per_device(groups, sites, right_vectors, left_vectors, vacancy):
    columns, piece = right_vectors.shape[1], right_vectors.shape[5]
    count_left, rows, width = left_vectors.shape[1:]
    shares = columns // (2 * COLS_AT_ONCE) * count_left
    fits = (
        piece % 128 == 0 and width % piece == 0 and right_vectors.shape[4] == 1
        and columns % (2 * COLS_AT_ONCE) == 0 and rows % 2 == 0 and rows >= HALO
        and sites >= 4 and sites % 2 == 0 and shares % (8 * sites) == 0 and count_left % 8 == 0 and (2 * count_left * rows) % 16 == 0
    )
    if fits:
        return per_device_fused(groups, sites, right_vectors, left_vectors, vacancy)
    return per_device_plain(right_vectors, left_vectors, vacancy)


def solution(mesh):
    return jax.shard_map(
        functools.partial(per_device, mesh.shape["cols"], mesh.shape["sites"]),
        mesh=mesh,
        in_specs=(
            P(None, None, None, None, ("cols", "sites"), None),
            P(None, None, "sites", None),
            P("sites", None),
        ),
        out_specs=P(None, None, None, None, "cols"),
        check_vma=False,
    )
```

```python
import functools

import jax
import jax.numpy as jnp
from jax import lax
from jax.experimental import pallas as pl
from jax.experimental.pallas import tpu as pltpu
from jax.sharding import PartitionSpec as P

MOM = 4


ONSITE_MASS = 0.3
SECOND_HOP = 0.2
BAND_SCALE = 4.5


def padded_2(cells, sides, width):
    for axis, dim in sides:
        count = lax.axis_size(axis)
        head = lax.slice_in_dim(cells, 0, width, axis=dim)
        tail = lax.slice_in_dim(cells, cells.shape[dim] - width, cells.shape[dim], axis=dim)
        cells = jnp.concatenate(
            [
                lax.ppermute(tail, axis, [(i, (i + 1) % count) for i in range(count)]),
                cells,
                lax.ppermute(head, axis, [((i + 1) % count, i) for i in range(count)]),
            ],
            axis=dim,
        )
    return cells


def column_shift(values, offset):
    row_width = values.shape[-1]
    filler = jnp.zeros(values.shape[:-1] + (abs(offset),), values.dtype)
    if offset > 0:
        return jnp.concatenate([values[..., offset:], filler], axis=-1)
    return jnp.concatenate([filler, values[..., : row_width + offset]], axis=-1)


def rotate_phase(values):
    return jnp.stack([-values[1], values[0]])


def sign_table(row_count, row_width):
    rows_index = lax.broadcasted_iota(jnp.int32, (row_count, row_width), 0)
    cols_index = lax.broadcasted_iota(jnp.int32, (row_count, row_width), 1)
    return (1 - 2 * ((rows_index + cols_index) % 2)).astype(jnp.float32)


def haldane(padded, parity_sign):
    centre = padded[:, :, 1:-1, :]
    upper_row = padded[:, :, 2:, :]
    lower_row = padded[:, :, :-2, :]
    vertical = jnp.where(parity_sign > 0, upper_row, lower_row)
    nearest = column_shift(centre, 1) + column_shift(centre, -1) + vertical
    second = (
        column_shift(centre, 2)
        - column_shift(centre, -2)
        + column_shift(upper_row, -1)
        - column_shift(lower_row, 1)
        + column_shift(lower_row, -1)
        - column_shift(upper_row, 1)
    )
    return (
        ONSITE_MASS * parity_sign * centre
        + nearest
        + SECOND_HOP * parity_sign * rotate_phase(second)
    )


def velocity(padded, parity_sign):
    centre = padded[:, :, 1:-1, :]
    upper_row = padded[:, :, 2:, :]
    lower_row = padded[:, :, :-2, :]
    along_x = column_shift(centre, 1) - column_shift(centre, -1)
    farther = column_shift(centre, 2) + column_shift(centre, -2)
    diagonal = (
        column_shift(upper_row, 1)
        + column_shift(upper_row, -1)
        + column_shift(lower_row, 1)
        + column_shift(lower_row, -1)
    )
    return rotate_phase(along_x) - SECOND_HOP * parity_sign * (2.0 * farther - diagonal)


def with_rims(values):
    return padded_2(values, (("sites", 2),), 1)


def per_device_plain(right_vectors, left_vectors, vacancy):
    layout = right_vectors.shape
    pieces = right_vectors.reshape(layout[0], layout[1], layout[2], layout[3], layout[5])
    slab_field = lax.all_to_all(
        lax.all_to_all(pieces, "cols", split_axis=2, concat_axis=2, tiled=True),
        "sites",
        split_axis=3,
        concat_axis=3,
        tiled=True,
    )
    row_count = left_vectors.shape[2]
    row_width = left_vectors.shape[3]
    count_left = left_vectors.shape[1]
    group_width = layout[1]
    site_count = row_count * row_width
    present = vacancy.astype(jnp.float32)
    current = slab_field.reshape(2, group_width, row_count, row_width) * present
    parity_sign = sign_table(row_count, row_width)
    latest = velocity(with_rims(current), parity_sign) * present
    previous = latest
    moment_list = [latest]
    for degree in range(1, MOM):
        applied = haldane(with_rims(latest), parity_sign) * present / BAND_SCALE
        following = applied if degree == 1 else 2.0 * applied - previous
        previous, latest = (latest, following)
        moment_list.append(latest)
    left_matrix = left_vectors.reshape(2 * count_left, site_count)
    summed_list = []
    for moment in moment_list:
        rounded = moment.astype(jnp.bfloat16).reshape(2 * group_width, site_count)
        product = lax.dot_general(
            left_matrix, rounded, (((1,), (1,)), ((), ())), preferred_element_type=jnp.float32
        ).reshape(2, count_left, 2, group_width)
        combined = jnp.stack(
            [product[0, :, 0] + product[1, :, 1], product[0, :, 1] - product[1, :, 0]]
        )
        summed_list.append(lax.psum(combined, "sites"))
    summed = jnp.stack(summed_list, axis=1)
    return summed[..., None]


MESH = pl.DeviceIdType.MESH
HALO = MOM
COLS_AT_ONCE = 16
LANES = 128


def fused_kernel(
    groups, sites, right_ref, left_ref, vacancy_ref, out_ref,
    arrived, field0, field1, field2, field3, present, scaled, doubled, rounded,
    staged, left_held, left_wide, left_flat, partial, shares, total,
    piece_send, piece_recv, rim_send, rim_recv, mask_send, mask_recv,
    share_send, share_recv, total_send, total_recv, left_sem, stage_sem,
):
    chunks, padded_rows, per_row, _, wide, piece = arrived.shape
    width = per_row * piece
    rows = padded_rows - 2 * HALO
    count = groups * sites
    my_group, my_site = lax.axis_index("cols"), lax.axis_index("sites")
    mine = my_group * sites + my_site
    above, below = lax.rem(my_site + 1, sites), lax.rem(my_site + sites - 1, sites)

    def piece_of(chunk, group, site):
        return right_ref.at[:, pl.ds(pl.multiple_of(chunk * wide, wide), wide), group, site, 0, :]

    def lay_out(chunk, carry):
        def place(other, inner):
            pltpu.make_async_copy(
                piece_of(chunk, other // sites, lax.rem(other, sites)), staged.at[chunk, other], stage_sem.at[chunk]
            ).start()
            return inner

        lax.fori_loop(0, count, place, 0)
        return carry

    left_copy = pltpu.make_async_copy(left_ref, left_held, left_sem)
    left_copy.start()
    barrier = pltpu.get_barrier_semaphore()

    def greet(step, carry):
        other = lax.rem(mine + step, count)
        pl.semaphore_signal(
            barrier, inc=1, device_id={"cols": other // sites, "sites": lax.rem(other, sites)}, device_id_type=MESH
        )
        return carry

    lax.fori_loop(1, count, greet, 0)
    lay_out(0, 0)

    for row in range(rows):
        present[HALO + row] = jnp.broadcast_to(vacancy_ref[row : row + 1, :].astype(jnp.float32), (8, width))

    pl.semaphore_wait(barrier, count - 1)

    def landing(chunk, run):
        return arrived.at[chunk, HALO + run // per_row, lax.rem(run, per_row)]

    def piece_copy(chunk, step):
        turn = lax.rem(step, 2) * (sites // 2) + step // (2 * groups)
        group = lax.rem(my_group + lax.rem(step // 2, groups), groups)
        site = lax.rem(my_site + turn, sites)
        return pltpu.make_async_remote_copy(
            src_ref=staged.at[chunk, group * sites + site],
            dst_ref=landing(chunk, mine),
            send_sem=piece_send.at[chunk, step],
            recv_sem=piece_recv.at[chunk],
            device_id={"cols": group, "sites": site},
            device_id_type=MESH,
        )

    def rim_copy(source, send_sem, recv_sem, up):
        first = rows if up else HALO
        landing_row = 0 if up else rows + HALO
        return pltpu.make_async_remote_copy(
            src_ref=source.at[pl.ds(first, HALO)],
            dst_ref=source.at[pl.ds(landing_row, HALO)],
            send_sem=send_sem,
            recv_sem=recv_sem,
            device_id={"sites": above if up else below},
            device_id_type=MESH,
        )

    def mask_copies():
        return [rim_copy(present, mask_send.at[i], mask_recv.at[i], up) for i, up in enumerate((True, False))]

    def rim_copies(chunk):
        return [
            rim_copy(arrived.at[chunk], rim_send.at[chunk, i], rim_recv.at[chunk, i], up)
            for i, up in enumerate((True, False))
        ]

    for copy in mask_copies():
        copy.start()

    def send_chunk(chunk, carry):
        pltpu.make_async_copy(staged.at[chunk], staged.at[chunk], stage_sem.at[chunk]).wait()

        def send(step, inner):
            piece_copy(chunk, step).start()
            return inner

        lax.fori_loop(1, count, send, 0)
        pltpu.make_async_copy(staged.at[chunk, mine], landing(chunk, mine), piece_recv.at[chunk]).start()
        return carry

    send_chunk(0, 0)
    lax.fori_loop(1, chunks, lay_out, 0)
    lax.fori_loop(1, min(2, chunks - 1), send_chunk, 0)

    for copy in mask_copies():
        copy.wait()

    def scale_masks(row, carry):
        held = present[row]
        scaled[row] = held * (1.0 / BAND_SCALE)
        doubled[row] = held * (2.0 / BAND_SCALE)
        return carry

    lax.fori_loop(0, padded_rows, scale_masks, 0)

    tiles = [slice(at, at + LANES) for at in range(0, width, LANES)]
    lane = lax.broadcasted_iota(jnp.int32, (8, LANES), 1)
    odd_lane = lax.rem(lane, 2) == 1
    even_sign = jnp.where(odd_lane, -1.0, 1.0)
    nothing = jnp.zeros((8, LANES), jnp.float32)

    def shift(values, offset):
        if offset > 0:
            turned = [pltpu.roll(v, LANES - 1, axis=1) for v in values]
            return [jnp.where(lane == LANES - 1, b, a) for a, b in zip(turned, turned[1:] + [nothing])]
        turned = [pltpu.roll(v, 1, axis=1) for v in values]
        return [jnp.where(lane == 0, b, a) for a, b in zip(turned, [nothing] + turned[:-1])]

    def sweep(source, target, earlier, mask, degree):
        first = degree + 1

        def one_row(row, odd_row):
            sign = -even_sign if odd_row else even_sign
            second, onsite = SECOND_HOP * sign, ONSITE_MASS * sign
            down = odd_lane != odd_row
            factor = [mask[row, :, at] for at in tiles]
            halves = [[], []]
            for part in range(0, wide, 8):
                eight = slice(part, part + 8)
                far, rest = [], []
                for r in (0, 1):
                    centre = [source[row, r, eight, at] for at in tiles]
                    upper = [source[row + 1, r, eight, at] for at in tiles]
                    lower = [source[row - 1, r, eight, at] for at in tiles]
                    right, left = shift(centre, 1), shift(centre, -1)
                    both = [u + l for u, l in zip(upper, lower)]
                    if degree == 0:
                        ahead = shift([2.0 * v - w for v, w in zip(right, both)], 1)
                        behind = shift([2.0 * v - w for v, w in zip(left, both)], -1)
                        far.append([second * (v + w) for v, w in zip(ahead, behind)])
                        rest.append([v - w for v, w in zip(right, left)])
                    else:
                        ahead = shift([v - w for v, w in zip(right, both)], 1)
                        behind = shift([v - w for v, w in zip(left, both)], -1)
                        far.append([second * (v - w) for v, w in zip(ahead, behind)])
                        rest.append([
                            (onsite * c + jnp.where(down, l, u)) + (v + w)
                            for c, u, l, v, w in zip(centre, upper, lower, right, left)
                        ])
                if degree == 0:
                    applied = [
                        [-v - w for v, w in zip(rest[1], far[0])],
                        [v - w for v, w in zip(rest[0], far[1])],
                    ]
                else:
                    applied = [
                        [v - w for v, w in zip(rest[0], far[1])],
                        [v + w for v, w in zip(rest[1], far[0])],
                    ]
                for r in (0, 1):
                    results = [v * f for v, f in zip(applied[r], factor)]
                    if earlier is not None:
                        results = [v - earlier[row, r, eight, at] for v, at in zip(results, tiles)]
                    if target is not None:
                        for v, at in zip(results, tiles):
                            target[row, r, eight, at] = v
                    halves[r].append(results)
            for r in (0, 1):
                base = (r * MOM + degree) * wide
                for i, at in enumerate(tiles):
                    lanes = pl.ds(pl.multiple_of(row * width + at.start, LANES), LANES)
                    block = jnp.concatenate([half[i] for half in halves[r]], axis=0)
                    rounded[base : base + wide, lanes] = block.astype(jnp.bfloat16)

        def pair(step, carry):
            one_row(first + 2 * step, first % 2 == 1)
            one_row(first + 2 * step + 1, first % 2 == 0)
            return carry

        lax.fori_loop(0, (padded_rows - 2 * first) // 2, pair, 0)

    left_copy.wait()

    def widen(step, carry):
        at = pl.ds(pl.multiple_of(step * 16, 16), 16)
        block = left_held[at, :].astype(jnp.float32)
        for i, lanes in enumerate(tiles):
            left_wide[i, at, :] = block[:, lanes]
        return carry

    lax.fori_loop(0, left_ref.shape[0] // 16, widen, 0)
    left_count = left_ref.shape[0] // rows
    for row in range(rows):
        for i, lanes in enumerate(tiles):
            block = left_wide[i, pl.ds(row, left_count, stride=rows), :]
            left_flat[:, row * width + lanes.start : row * width + lanes.stop] = block.astype(jnp.bfloat16)

    def stage(chunk):
        held = arrived.at[chunk, pl.ds(HALO, rows)]
        pltpu.make_async_copy(held, held, piece_recv.at[chunk]).wait()
        for copy in rim_copies(chunk):
            copy.start()

        @pl.when(chunk + 2 < chunks - 1)
        def _():
            send_chunk(chunk + 2, 0)

        @pl.when(chunk == chunks - 2)
        def _():
            send_chunk(chunks - 1, 0)

    def compute(chunk):
        for copy in rim_copies(chunk):
            copy.wait()

        def mask_row(row, carry):
            for r in (0, 1):
                for part in range(0, wide, 8):
                    at = slice(part, part + 8)
                    for run in range(per_row):
                        lanes = slice(run * piece, (run + 1) * piece)
                        field0[row, r, at, lanes] = arrived[chunk, row, run, r, at, :] * present[row, :, lanes]
            return carry

        lax.fori_loop(0, padded_rows, mask_row, 0)
        sweep(field0, field1, None, present, 0)
        sweep(field1, field2, None, scaled, 1)
        sweep(field2, field3, field1, doubled, 2)
        sweep(field3, None, field2, doubled, 3)
        product = lax.dot_general(
            left_flat[...],
            rounded[:, HALO * width : (HALO + rows) * width],
            (((1,), (1,)), ((), ())),
            preferred_element_type=jnp.float32,
        )
        count_left = product.shape[0] // 2
        half = product.shape[1] // 2
        real, imaginary = product[:count_left], product[count_left:]
        swapped = pltpu.roll(imaginary, half, axis=1)
        wheres = lax.broadcasted_iota(jnp.int32, swapped.shape, 1)
        combined = real + jnp.where(wheres < half, swapped, -swapped)
        partial[pl.ds(pl.multiple_of(chunk * count_left, count_left), count_left), :] = combined

    def step_chunk(step, carry):
        stage(step)

        def work(chunk, inner):
            compute(chunk)
            return inner

        start = jnp.where(step < chunks - 1, jnp.maximum(step - 1, 0), step)
        lax.fori_loop(start, jnp.where(step < chunks - 2, step, step + 1), work, 0)
        return carry

    lax.fori_loop(0, chunks, step_chunk, 0)

    share_rows = shares.shape[1]

    def rows_of(site):
        return pl.ds(pl.multiple_of(site * share_rows, share_rows), share_rows)

    def share_copy(step):
        site = lax.rem(my_site + step, sites)
        return pltpu.make_async_remote_copy(
            src_ref=partial.at[rows_of(site)],
            dst_ref=shares.at[my_site],
            send_sem=share_send.at[step],
            recv_sem=share_recv,
            device_id={"sites": site},
            device_id_type=MESH,
        )

    def total_copy(step):
        site = lax.rem(my_site + step, sites)
        return pltpu.make_async_remote_copy(
            src_ref=total.at[rows_of(my_site)],
            dst_ref=total.at[rows_of(my_site)],
            send_sem=total_send.at[step],
            recv_sem=total_recv,
            device_id={"sites": site},
            device_id_type=MESH,
        )

    def start_all(make, stop):
        def go(step, carry):
            make(step).start()
            return carry

        lax.fori_loop(1, stop, go, 0)

    def sent_all(make, stop):
        def go(step, carry):
            make(step).wait_send()
            return carry

        lax.fori_loop(1, stop, go, 0)

    start_all(share_copy, sites)
    pltpu.make_async_copy(partial.at[rows_of(my_site)], shares.at[my_site], share_recv).start()
    pltpu.make_async_copy(shares, shares, share_recv).wait()
    summed = shares[0]
    for site in range(1, sites):
        summed = summed + shares[site]
    total[rows_of(my_site), :] = summed
    start_all(total_copy, sites)
    whole = total.at[pl.ds(0, (sites - 1) * share_rows)]
    pltpu.make_async_copy(whole, whole, total_recv).wait()
    out_ref[...] = total[...]
    sent_all(share_copy, sites)
    sent_all(total_copy, sites)

    def sent_chunk(chunk, carry):
        sent_all(functools.partial(piece_copy, chunk), count)
        return carry

    lax.fori_loop(0, chunks, sent_chunk, 0)


def per_device_fused(groups, sites, right_vectors, left_vectors, vacancy):
    width_group, piece = right_vectors.shape[1], right_vectors.shape[5]
    count_left, rows, width = left_vectors.shape[1:]
    wide = COLS_AT_ONCE
    chunks = width_group // wide
    padded = rows + 2 * HALO
    field = pltpu.VMEM((padded, 2, wide, width), jnp.float32)
    mask = pltpu.VMEM((padded, 8, width), jnp.float32)
    sums = (chunks * count_left, 2 * MOM * wide)
    dma = pltpu.SemaphoreType.DMA
    call = pl.pallas_call(
        functools.partial(fused_kernel, groups, sites),
        out_shape=jax.ShapeDtypeStruct(sums, jnp.float32),
        in_specs=[
            pl.BlockSpec(memory_space=pltpu.HBM),
            pl.BlockSpec(memory_space=pltpu.HBM),
            pl.BlockSpec(memory_space=pltpu.VMEM),
        ],
        out_specs=pl.BlockSpec(memory_space=pltpu.VMEM),
        scratch_shapes=[
            pltpu.VMEM((chunks, padded, width // piece, 2, wide, piece), jnp.float32),
            field, field, field, field, mask, mask, mask,
            pltpu.VMEM((2 * MOM * wide, padded * width), jnp.bfloat16),
            pltpu.VMEM((chunks, groups * sites, 2, wide, piece), jnp.float32),
            pltpu.VMEM((2 * count_left * rows, width), jnp.bfloat16),
            pltpu.VMEM((width // LANES, 2 * count_left * rows, LANES), jnp.float32),
            pltpu.VMEM((2 * count_left, rows * width), jnp.bfloat16),
            pltpu.VMEM(sums, jnp.float32),
            pltpu.VMEM((sites, sums[0] // sites, sums[1]), jnp.float32),
            pltpu.VMEM(sums, jnp.float32),
            dma((chunks, groups * sites)), dma((chunks,)),
            dma((chunks, 2)), dma((chunks, 2)), dma((2,)), dma((2,)),
            dma((sites,)), dma, dma((sites,)), dma, dma, dma((chunks,)),
        ],
        compiler_params=pltpu.CompilerParams(
            collective_id=0, has_side_effects=True, vmem_limit_bytes=125 * 512 * 1024
        ),
        cost_estimate=pl.CostEstimate(flops=2 * 10**9, bytes_accessed=8 * 10**6, transcendentals=0),
    )
    summed = call(right_vectors, left_vectors.reshape(2 * count_left * rows, width), vacancy)
    summed = summed.reshape(chunks, count_left, 2, MOM, wide)
    return summed.transpose(2, 3, 1, 0, 4).reshape(2, MOM, count_left, width_group, 1)


def per_device(groups, sites, right_vectors, left_vectors, vacancy):
    columns, piece = right_vectors.shape[1], right_vectors.shape[5]
    count_left, rows, width = left_vectors.shape[1:]
    shares = (columns // COLS_AT_ONCE) * count_left
    fits = (
        piece % 128 == 0 and width % piece == 0 and right_vectors.shape[4] == 1
        and columns % COLS_AT_ONCE == 0 and rows % 2 == 0 and rows >= HALO
        and sites >= 4 and columns >= 2 * COLS_AT_ONCE and sites % 2 == 0 and shares % (8 * sites) == 0 and count_left % 8 == 0 and (2 * count_left * rows) % 16 == 0
    )
    if fits:
        return per_device_fused(groups, sites, right_vectors, left_vectors, vacancy)
    return per_device_plain(right_vectors, left_vectors, vacancy)


def solution(mesh):
    return jax.shard_map(
        functools.partial(per_device, mesh.shape["cols"], mesh.shape["sites"]),
        mesh=mesh,
        in_specs=(
            P(None, None, None, None, ("cols", "sites"), None),
            P(None, None, "sites", None),
            P("sites", None),
        ),
        out_specs=P(None, None, None, None, "cols"),
        check_vma=False,
    )
```
